512 devices in a mesh: slab: 8 (over x, core), coil: 16 (over z_lo, y), row: 4 (over z_hi).
Axes of the slice: x: 4, y: 8, z: 8 (z_hi: 4, z_lo: 2; z = z_hi * 2 + z_lo), core: 2. Of those that a mesh axis runs over, the one named last changes fastest.
Arguments:
- solution: float32 [2, 8, 384, 384], P(None, 'slab', 'row'), may hold values from -6 to 6
- residual: float32 [2, 8, 384, 384], P(None, 'slab', 'row'), may hold values from -90 to 90
- direction: float32 [2, 8, 384, 384], P(None, 'slab', 'row'), may hold values from -90 to 90
- sens: bfloat16 [2, 32, 8, 384, 384], P(None, 'coil', 'slab', 'row'), may hold values from -0.75 to 0.75
- sample_cell: int32 [2048], P('row'), may hold values from 0 to 36863
- kernel: float32 [2, 5, 2048], P(None, None, 'row'), may hold values from 0.2 to 1
- density: float32 [2048], P('row'), may hold values from 0.5 to 4
Outputs:
- solution_next: float32 [2, 8, 384, 384], P(None, 'slab', 'row')
- residual_next: float32 [2, 8, 384, 384], P(None, 'slab', 'row')
- direction_next: float32 [2, 8, 384, 384], P(None, 'slab', 'row')
The draws below stay inside these ranges and needn't reach their ends.
All inputs are finite; a program needn't handle non-finite values.
Results may differ from the reference program's by a relative error of at most 0.0003.
Values sent between devices are 32-bit elements; how exact they have to be, the bound alone decides.
A program may use at most 64 MiB of HBM per device.

```python
import math
import jax
import jax.numpy as jnp
from jax import lax

NXY = 384
KW = 5
SAMP_DEV = 512
COILS = 32
Z = 8
BAND = 96
NSAMP = 2048


def field_scales(key, salt):
    row_key, col_key = jax.random.split(jax.random.fold_in(key, salt))
    row_scale = 10.0 ** jax.random.uniform(row_key, (NXY,), jnp.float32)
    col_scale = 10.0 ** jax.random.uniform(col_key, (NXY,), jnp.float32)
    position = (jnp.arange(Z)[:, None] * NXY + jnp.arange(NXY)[None, :]).astype(jnp.float32) / (Z * NXY)
    ramp = 3.0 ** (0.5 * position)
    return 0.1 * ramp[None, :, :, None] * row_scale[None, None, :, None] * col_scale[None, None, None, :]


def draw_residual(key, part):
    base_key = jax.random.fold_in(jax.random.fold_in(key, 11), 0)
    base = jax.random.truncated_normal(base_key, -4.0, 4.0, (2, Z, NXY, NXY), jnp.float32)
    return base * field_scales(key, 13)


def draw_direction(key, part):
    base_key = jax.random.fold_in(jax.random.fold_in(key, 21), 0)
    base = jax.random.truncated_normal(base_key, -4.0, 4.0, (2, Z, NXY, NXY), jnp.float32)
    return base * field_scales(key, 23)


def touch_ends(array, key, low, high):
    extent = array.shape
    place = [jax.random.randint(jax.random.fold_in(key, axis), (), 0, extent[axis]) for axis in range(len(extent))]
    array = array.at[tuple(place)].set(low)
    longest = extent.index(max(extent))
    place[longest] = (place[longest] + 1) % extent[longest]
    return array.at[tuple(place)].set(high)


def block_levels(own_key, dims, cuts, smallest, largest):
    def one(dim, shards_of):
        draws = jax.random.uniform(jax.random.fold_in(jax.random.fold_in(own_key, 6), dim), (shards_of,), jnp.float32, smallest / len(cuts), largest / len(cuts))
        return jnp.repeat(jnp.exp(draws), dims[dim] // shards_of).reshape((-1,) + (1,) * (len(dims) - dim - 1))

    loudness = one(*cuts[0])
    for cut in cuts[1:]:
        loudness = loudness * one(*cut)
    return loudness


def normal_values(rng, extent, deviation, bound, pieces=(), held_as=jnp.bfloat16):
    factor_of = block_levels(rng, extent, pieces, -0.22, 0.18) if pieces else 1.0
    entries = jax.random.normal(rng, extent, jnp.float32) * deviation * factor_of
    return jnp.minimum(jnp.maximum(entries, -bound), bound).astype(held_as)


def setup_inputs(seed: int = 0) -> dict:
    key_of = jax.random.split(jax.random.key(seed), 8)
    return {
        "solution": normal_values(key_of[0], (2, Z, NXY, NXY), 1.0, 6.0, ((1, 8), (2, 4)), jnp.float32),
        "residual": draw_residual(jax.random.fold_in(key_of[7], 71), 0),
        "direction": draw_direction(jax.random.fold_in(key_of[7], 71), 0),
        "sens": normal_values(key_of[3], (2, COILS, Z, NXY, NXY), (2 * COILS) ** -0.5, 0.75, ((1, 16), (2, 8), (3, 4))),
        "sample_cell": touch_ends(jax.random.randint(key_of[4], (NSAMP,), 0, BAND * NXY), jax.random.fold_in(key_of[4], 1), 0, (BAND * NXY) - 1).astype(jnp.int32),
        "kernel": jnp.clip(jnp.exp(math.log(1.0) - 1.609438 * jax.random.uniform(key_of[5], (2, KW, NSAMP), jnp.float32) ** block_levels(key_of[5], (2, KW, NSAMP), ((2, 4),), -0.2, 0.2)), 0.2, 1.0),
        "density": jnp.clip(jnp.exp(math.log(4.0) - 2.0794415 * jax.random.uniform(key_of[6], (NSAMP,), jnp.float32) ** block_levels(key_of[6], (NSAMP,), ((0, 4),), -0.2, 0.2)), 0.5, 4.0),
    }


damping = 0.05


def reference(solution, residual, direction, sens, sample_cell, kernel, density):
    sample_ids = jnp.arange(NSAMP, dtype=jnp.int32)
    sample_col = (sample_ids // SAMP_DEV) * BAND + sample_cell // NXY
    sample_row = sample_cell % NXY
    half_taps = KW // 2

    def coil_step(running, coil_sens):
        sens_float = coil_sens.astype(jnp.float32)
        coil_image = (sens_float[0] * direction[0] - sens_float[1] * direction[1]) + 1j * (sens_float[0] * direction[1] + sens_float[1] * direction[0])
        coil_image = 0.5 * (coil_image + jnp.roll(coil_image, Z // 2, axis=0))
        kspace = jnp.fft.fft2(coil_image, axes=(1, 2), norm="ortho")
        values = jnp.zeros((Z, NSAMP), kspace.dtype)
        for row_tap in range(KW):
            for col_tap in range(KW):
                rows_at = (sample_row + row_tap - half_taps) % NXY
                cols_at = (sample_col + col_tap - half_taps) % NXY
                values = values + (kernel[0, row_tap] * kernel[1, col_tap]) * kspace[:, rows_at, cols_at]
        weighted = values * density
        spread = jnp.zeros_like(kspace)
        for row_tap in range(KW):
            for col_tap in range(KW):
                rows_at = (sample_row + row_tap - half_taps) % NXY
                cols_at = (sample_col + col_tap - half_taps) % NXY
                spread = spread.at[:, rows_at, cols_at].add((kernel[0, row_tap] * kernel[1, col_tap]) * weighted)
        returned = jnp.fft.ifft2(spread, axes=(1, 2), norm="ortho")
        coil_term = jnp.conj(sens_float[0] + 1j * sens_float[1]) * returned
        return running + jnp.stack([jnp.real(coil_term), jnp.imag(coil_term)]), None

    coil_sum, unused = lax.scan(coil_step, jnp.zeros_like(direction), jnp.moveaxis(sens, 1, 0))
    normal_image = coil_sum + damping * direction
    norm_now = jnp.sum(residual * residual)
    curvature = jnp.sum(direction * normal_image)
    step_length = norm_now / curvature
    solution_next = solution + step_length * direction
    residual_next = residual - step_length * normal_image
    norm_next = jnp.sum(residual_next * residual_next)
    direction_next = residual_next + (norm_next / norm_now) * direction
    return (solution_next, residual_next, direction_next)
```

```python
import functools
import math

import jax
import jax.numpy as jnp
import ml_dtypes
import numpy as np
from jax import lax
from jax.experimental import pallas as pl
from jax.experimental.pallas import tpu as pltpu
from jax.sharding import PartitionSpec as P

damping = 0.05
NXY = 384
BAND = 96
EXT = 128
HALO = 2
SAMP = 512
TAPS = 5
BLOCKS = 3
F32 = jnp.float32
BF16 = jnp.bfloat16
MESH = pl.DeviceIdType.MESH


def split_table(table):
    high = table.astype(np.float32).astype(ml_dtypes.bfloat16)
    low = (table - high.astype(np.float64)).astype(np.float32).astype(ml_dtypes.bfloat16)
    return high, low


def transform_tables(bands):
    x = np.arange(NXY)
    forward = np.zeros((bands, 2 * NXY, 2 * EXT))
    inverse = np.zeros((BLOCKS, bands * 2 * EXT, 256))
    scale = 1.0 / math.sqrt(NXY)
    for band in range(bands):
        k = (band * BAND - HALO + np.arange(EXT)) % NXY
        angle = (x[:, None] * k[None, :] % NXY) * (2.0 * math.pi / NXY)
        cosine, sine = np.cos(angle) * scale, np.sin(angle) * scale
        forward[band] = np.block([[cosine, -sine], [sine, cosine]])
        back = np.block([[cosine.T, sine.T], [-sine.T, cosine.T]])
        rows = slice(band * 2 * EXT, (band + 1) * 2 * EXT)
        for block in range(BLOCKS):
            cols = slice(block * 128, (block + 1) * 128)
            inverse[block, rows, :128] = back[:, :NXY][:, cols]
            inverse[block, rows, 128:] = back[:, NXY:][:, cols]
    return split_table(forward) + split_table(inverse)


def halves(value):
    high = value.astype(BF16)
    return high, (value - high.astype(F32)).astype(BF16)


def fold_phase(index):
    turn = index - NXY * jnp.floor(index * (1.0 / NXY) + 0.5)
    size = jnp.abs(turn)

    def sine_quarter(u):
        t = u * (2.0 * math.pi / NXY)
        q = t * t
        p = 1.0 / 6227020800.0
        for c in (-1.0 / 39916800.0, 1.0 / 362880.0, -1.0 / 5040.0, 1.0 / 120.0, -1.0 / 6.0, 1.0):
            p = p * q + c
        return p * t

    quarter = NXY // 4
    cosine = sine_quarter(quarter - size)
    sine = sine_quarter(quarter - jnp.abs(size - quarter))
    return cosine, jnp.where(turn < 0.0, -sine, sine)


def dot(a, b):
    return lax.dot_general(a, b, (((1,), (0,)), ((), ())), preferred_element_type=F32)


def dot_nt(a, b):
    return lax.dot_general(a, b, (((1,), (1,)), ((), ())), preferred_element_type=F32)


def kernel(
    rows_n, groups_n, ys_n,
    dir_ref, res_ref, sens_ref, cell_ref, kern_ref, dens_ref,
    fh_ref, fl_ref, bh_ref, bl_ref,
    n_ref, scal_ref,
    lhs_h, lhs_l, ke_h, ke_l, sinfo, cw, wr, tbuf, yconst, a_h, a_l, s_h, s_l,
    vsend, vrecv, wall, tz, zrecv, yrecv, ysum, nbuf, rz,
    g1, z1, y1, e2, g2, z2, y2,
    info_s, info_r, val_s, val_r, wt_s, wt_r,
    g1_s, g1_r, z1_s, z1_r, y1_s, y1_r,
    e2_s, e2_r, g2_s, g2_r, z2_s, z2_r, y2_s, y2_r,
    zr_s, zr_r, yr_s, yr_r, ya_s, ya_r, za_s, za_r,
):
    slab = lax.axis_index("slab")
    coil = lax.axis_index("coil")
    row = lax.axis_index("row")
    pair = slab // groups_n
    group = slab % groups_n
    zl = coil // ys_n
    yy = coil % ys_n
    half = SAMP // 128

    def remote(src, dst, send, recv, slab_to=None, coil_to=None, row_to=None):
        target = (
            slab if slab_to is None else slab_to,
            coil if coil_to is None else coil_to,
            row if row_to is None else row_to,
        )
        copy = pltpu.make_async_remote_copy(
            src_ref=src, dst_ref=dst, send_sem=send, recv_sem=recv,
            device_id=target, device_id_type=MESH,
        )
        copy.start()
        started.append(copy)
        return copy

    started = []

    eight = [(k, e) for k in range(rows_n) for e in range(2) if (k, e) != (0, 0)]

    def eight_to(k, e):
        return (group + groups_n * ((pair + e) % 2), (row + k) % rows_n)

    barrier = pltpu.get_barrier_semaphore()
    count = 0
    for k, e in eight:
        s, r = eight_to(k, e)
        pl.semaphore_signal(barrier, inc=1, device_id=(s, coil, r), device_id_type=MESH)
        count += 1
    for k in range(1, groups_n):
        s = (group + k) % groups_n + groups_n * pair
        pl.semaphore_signal(barrier, inc=1, device_id=(s, coil, row), device_id_type=MESH)
        count += 1
    pl.semaphore_signal(
        barrier, inc=1, device_id=(slab, (1 - zl) * ys_n + yy, row), device_id_type=MESH
    )
    count += 1
    for k in range(1, ys_n):
        c = zl * ys_n + (yy + k) % ys_n
        pl.semaphore_signal(barrier, inc=1, device_id=(slab, c, row), device_id_type=MESH)
        count += 1

    cell = cell_ref[...].astype(F32)
    kx = jnp.floor((cell + 0.5) * (1.0 / NXY))
    sinfo[row, 0:5, :] = kern_ref[0]
    sinfo[row, 5:10, :] = kern_ref[1]
    sinfo[row, 10:11, :] = cell - NXY * kx
    sinfo[row, 11:12, :] = kx

    pl.semaphore_wait(barrier, count)
    info = [None] + [
        remote(sinfo.at[row], sinfo.at[row], info_s.at[k], info_r.at[k], row_to=(row + k) % rows_n)
        for k in range(1, rows_n)
    ]

    for c in range(2):
        sr, si = sens_ref[0, c].astype(F32), sens_ref[1, c].astype(F32)
        dr, di = dir_ref[0], dir_ref[1]
        re_h, re_l = halves(sr * dr - si * di)
        im_h, im_l = halves(sr * di + si * dr)
        here = slice(c * BAND, (c + 1) * BAND)
        lhs_h[here, 0:NXY] = re_h
        lhs_h[here, NXY:] = im_h
        lhs_l[here, 0:NXY] = re_l
        lhs_l[here, NXY:] = im_l

    for band in range(rows_n):
        out = dot(lhs_h[...], fh_ref[band])
        out = out + dot(lhs_l[...], fh_ref[band])
        out = out + dot(lhs_h[...], fl_ref[band])
        high, low = halves(out)
        ke_h[band, 0:192] = high[:, :EXT]
        ke_h[band, 192:384] = high[:, EXT:]
        ke_l[band, 0:192] = low[:, :EXT]
        ke_l[band, 192:384] = low[:, EXT:]

    first = (row * BAND).astype(F32)
    ypos = lax.broadcasted_iota(jnp.int32, (BAND, 128), 0).astype(F32) + first
    c1, s1 = fold_phase(ypos)
    yconst[0] = c1
    yconst[1] = s1
    yconst[2] = 2.0 * c1 * c1 - 1.0
    yconst[3] = 2.0 * s1 * c1

    for b in range(BLOCKS):
        for plane in range(2):
            for g in range(24):
                rz[b, plane, g] = res_ref[plane, 4 * g : 4 * g + 4, 128 * b : 128 * (b + 1)]

    def wide(tile):
        return jnp.concatenate([tile] * half, axis=1)

    vals = {}
    for k in range(rows_n):
        band = (row + k) % rows_n
        if k:
            info[rows_n - k].wait_recv()
        ky = sinfo[band, 10:11, :]
        kxs = sinfo[band, 11:12, :]
        k0 = [sinfo[band, t : t + 1, :] for t in range(TAPS)]
        k1 = [sinfo[band, 5 + t : 6 + t, :] for t in range(TAPS)]
        cells = lax.broadcasted_iota(jnp.int32, (16, SAMP), 0).astype(F32)
        for g in range(8):
            if g < 7:
                offset = cells + (16.0 * g) - kxs
                weight = jnp.where(offset == 4.0, k1[4], 0.0)
                for t in range(3, -1, -1):
                    weight = jnp.where(offset == float(t), k1[t], weight)
                high, low = halves(weight)
            else:
                high = low = jnp.zeros((16, SAMP), BF16)
            cw[k, 16 * g : 16 * g + 16] = high
            cw[k, EXT + 16 * g : EXT + 16 * g + 16] = low
        low_pos = lax.broadcasted_iota(jnp.int32, (8, SAMP), 0).astype(F32)
        lo_c, lo_s = fold_phase(low_pos * ky)
        lo_c = lo_c * (1.0 / math.sqrt(NXY))
        lo_s = lo_s * (1.0 / math.sqrt(NXY))
        high_pos = lax.broadcasted_iota(jnp.int32, (16, SAMP), 0).astype(F32) * 8.0 + first
        hi_c, hi_s = fold_phase(high_pos * ky)
        even1, odd1 = k0[3] + k0[1], k0[3] - k0[1]
        even2, odd2 = k0[4] + k0[0], k0[4] - k0[0]
        for p in range(BAND // 8):
            r8 = slice(8 * p, 8 * p + 8)
            pr = k0[2] + even1 * wide(yconst[0, r8]) + even2 * wide(yconst[2, r8])
            pi = odd1 * wide(yconst[1, r8]) + odd2 * wide(yconst[3, r8])
            hc, hs = hi_c[p : p + 1], hi_s[p : p + 1]
            er = hc * lo_c - hs * lo_s
            es = hs * lo_c + hc * lo_s
            wr[k, 0, r8] = er * pr - es * pi
            wr[k, 1, r8] = er * pi + es * pr
        kh, kl = ke_h[band], ke_l[band]
        tbuf[...] = dot(jnp.concatenate([kh, kh], axis=1), cw[k]) + dot(kl, cw[k, 0:EXT])
        for c in range(2):
            vr = jnp.zeros((8, SAMP), F32)
            vi = jnp.zeros((8, SAMP), F32)
            for p in range(BAND // 8):
                tr = tbuf[c * BAND + 8 * p : c * BAND + 8 * p + 8]
                ti = tbuf[192 + c * BAND + 8 * p : 192 + c * BAND + 8 * p + 8]
                w_r, w_i = wr[k, 0, 8 * p : 8 * p + 8], wr[k, 1, 8 * p : 8 * p + 8]
                vr = vr + w_r * tr + w_i * ti
                vi = vi + w_r * ti - w_i * tr
            vr = jnp.sum(vr, axis=0, keepdims=True)
            vi = jnp.sum(vi, axis=0, keepdims=True)
            for b in range(half):
                vsend[k, c, b : b + 1] = vr[:, 128 * b : 128 * (b + 1)]
                vsend[k, c, half + b : half + b + 1] = vi[:, 128 * b : 128 * (b + 1)]
        for e in range(2):
            if (k, e) == (0, 0):
                continue
            c = (pair + e) % 2
            s, r = eight_to(k, e)
            vals[k, e] = remote(
                vsend.at[k, c], vrecv.at[k, e], val_s.at[k, e], val_r.at[k, e], slab_to=s, row_to=r
            )

    total = vsend[0, pair]
    for k, e in eight:
        vals[k, e].wait_recv()
        total = total + vrecv[k, e]
    value = 0.5 * total
    dens = dens_ref[...]
    weighted = value * jnp.concatenate([dens, dens], axis=0)
    wall[row, pair, 0:8] = weighted
    curv = jnp.sum(weighted * value, axis=0, keepdims=True) * 2.0
    coils = 2 * ys_n

    def lanes(tile):
        folded = tile[:, 0:128] + tile[:, 128:256] + tile[:, 256:384]
        return jnp.sum(folded, axis=0, keepdims=True)

    dd = lanes(dir_ref[0] * dir_ref[0] + dir_ref[1] * dir_ref[1])
    rr = lanes(res_ref[0] * res_ref[0] + res_ref[1] * res_ref[1])
    wall[row, pair, 8:9] = curv + dd * (damping / coils)
    wall[row, pair, 9:10] = rr * (1.0 / coils)
    wall[row, pair, 10:16] = jnp.zeros((6, 128), F32)
    wts = {}
    for k, e in eight:
        s, r = eight_to(k, e)
        wts[k, e] = remote(
            wall.at[row, pair], wall.at[row, pair], wt_s.at[k, e], wt_r.at[k, e], slab_to=s, row_to=r
        )

    for k in range(rows_n):
        band = (row + k) % rows_n
        for e in range(2):
            if (k, e) != (0, 0):
                wts[(rows_n - k) % rows_n, e].wait_recv()
        for c in range(2):
            w_re = jnp.concatenate([wall[band, c, b : b + 1] for b in range(half)], axis=1)
            w_im = jnp.concatenate([wall[band, c, half + b : half + b + 1] for b in range(half)], axis=1)
            for p in range(BAND // 16):
                m_r = wr[k, 0, 16 * p : 16 * p + 16]
                m_i = wr[k, 1, 16 * p : 16 * p + 16]
                re_h, re_l = halves(m_r * w_re - m_i * w_im)
                im_h, im_l = halves(m_r * w_im + m_i * w_re)
                here = slice(c * BAND + 16 * p, c * BAND + 16 * p + 16)
                there = slice(192 + c * BAND + 16 * p, 192 + c * BAND + 16 * p + 16)
                a_h[here] = re_h
                a_h[there] = im_h
                a_l[here] = re_l
                a_l[there] = im_l
        both = dot_nt(a_h[...], cw[k])
        out = both[:, :EXT] + both[:, EXT:] + dot_nt(a_l[...], cw[k, 0:EXT])
        high, low = halves(out)
        s_h[band, 0] = high[0:192]
        s_h[band, 1] = high[192:384]
        s_l[band, 0] = low[0:192]
        s_l[band, 1] = low[192:384]

    mine = jnp.zeros((8, 128), F32)
    for r in range(rows_n):
        for c in range(2):
            mine = mine + wall[r, c, 8:16]
    g1[group] = mine
    g1c = [
        remote(g1.at[group], g1.at[group], g1_s.at[k], g1_r.at[k],
               slab_to=(group + k) % groups_n + groups_n * pair)
        for k in range(1, groups_n)
    ]

    left_h = jnp.concatenate([s_h[j, q] for j in range(rows_n) for q in range(2)], axis=1)
    left_l = jnp.concatenate([s_l[j, q] for j in range(rows_n) for q in range(2)], axis=1)
    other = (1 - zl) * ys_n + yy
    zrc = []
    for b in range(BLOCKS):
        out = dot(left_h, bh_ref[b]) + dot(left_l, bh_ref[b]) + dot(left_h, bl_ref[b])
        cols = slice(128 * b, 128 * (b + 1))
        term_r = dir_ref[0, :, cols] * (damping / coils)
        term_i = dir_ref[1, :, cols] * (damping / coils)
        for c in range(2):
            sr = sens_ref[0, c, :, cols].astype(F32)
            si = sens_ref[1, c, :, cols].astype(F32)
            br = out[c * BAND : (c + 1) * BAND, :128]
            bi = out[c * BAND : (c + 1) * BAND, 128:]
            term_r = term_r + sr * br + si * bi
            term_i = term_i + sr * bi - si * br
        for g in range(24):
            tz[b, 0, g] = term_r[4 * g : 4 * g + 4]
            tz[b, 1, g] = term_i[4 * g : 4 * g + 4]
        zrc.append(remote(tz.at[b, 1 - zl], zrecv.at[b], zr_s.at[b], zr_r.at[b], coil_to=other))

    for copy in g1c:
        copy.wait_recv()
    mine = g1[0]
    for k in range(1, groups_n):
        mine = mine + g1[k]
    z1[zl] = mine
    z1c = remote(z1.at[zl], z1.at[zl], z1_s, z1_r, coil_to=other)

    yrc = {}
    for b in range(BLOCKS):
        zrc[b].wait_recv()
        ysum[b] = tz[b, zl] + zrecv[b]
        for k in range(1, ys_n):
            to = (yy + k) % ys_n
            yrc[b, k] = remote(
                ysum.at[b, pl.ds(3 * to, 3)], yrecv.at[b, k], yr_s.at[b, k], yr_r.at[b, k],
                coil_to=zl * ys_n + to,
            )
        if b == 0:
            z1c.wait_recv()
            y1[yy] = z1[0] + z1[1]
            y1c = [
                remote(y1.at[yy], y1.at[yy], y1_s.at[k], y1_r.at[k], coil_to=zl * ys_n + (yy + k) % ys_n)
                for k in range(1, ys_n)
            ]
    for copy in y1c:
        copy.wait_recv()
    mine = y1[0]
    for k in range(1, ys_n):
        mine = mine + y1[k]
    curvature = jnp.sum(mine[0:1], axis=1, keepdims=True)
    norm_now = jnp.sum(mine[1:2], axis=1, keepdims=True)
    step = norm_now / curvature

    left = jnp.zeros((4, 128), F32)
    yac = {}
    for b in range(BLOCKS):
        for k in range(1, ys_n):
            yrc[b, k].wait_recv()
        for g in range(3):
            acc = ysum[b, 3 * yy + g]
            for k in range(1, ys_n):
                acc = acc + yrecv[b, k, g]
            nbuf[b, zl, 3 * yy + g] = acc
            gap = rz[b, zl, 3 * yy + g] - step * acc
            left = left + gap * gap
        piece = nbuf.at[b, zl, pl.ds(3 * yy, 3)]
        for k in range(1, ys_n):
            yac[b, k] = remote(
                piece, piece, ya_s.at[b, k], ya_r.at[b, k], coil_to=zl * ys_n + (yy + k) % ys_n
            )
    left = jnp.sum(left, axis=0, keepdims=True)
    e2[row, pair] = jnp.broadcast_to(left, (8, 128))
    e2c = {}
    for k, e in eight:
        s, r = eight_to(k, e)
        e2c[k, e] = remote(
            e2.at[row, pair], e2.at[row, pair], e2_s.at[k, e], e2_r.at[k, e], slab_to=s, row_to=r
        )
    for k, e in eight:
        e2c[k, e].wait_recv()
    mine = jnp.zeros((8, 128), F32)
    for r in range(rows_n):
        for c in range(2):
            mine = mine + e2[r, c]
    g2[group] = mine
    g2c = [
        remote(g2.at[group], g2.at[group], g2_s.at[k], g2_r.at[k],
               slab_to=(group + k) % groups_n + groups_n * pair)
        for k in range(1, groups_n)
    ]

    zac = []
    for b in range(BLOCKS):
        for k in range(1, ys_n):
            yac[b, k].wait_recv()
        part = nbuf.at[b, zl]
        zac.append(remote(part, part, za_s.at[b], za_r.at[b], coil_to=other))

    for copy in g2c:
        copy.wait_recv()
    mine = g2[0]
    for k in range(1, groups_n):
        mine = mine + g2[k]
    z2[zl] = mine
    z2c = remote(z2.at[zl], z2.at[zl], z2_s, z2_r, coil_to=other)
    z2c.wait_recv()
    y2[yy] = z2[0] + z2[1]
    y2c = [
        remote(y2.at[yy], y2.at[yy], y2_s.at[k], y2_r.at[k], coil_to=zl * ys_n + (yy + k) % ys_n)
        for k in range(1, ys_n)
    ]
    for copy in y2c:
        copy.wait_recv()
    mine = y2[0]
    for k in range(1, ys_n):
        mine = mine + y2[k]
    norm_next = jnp.sum(mine[0:1], axis=1, keepdims=True)
    scal_ref[0:1] = jnp.broadcast_to(step, (1, 128))
    scal_ref[1:2] = jnp.broadcast_to(norm_next / norm_now, (1, 128))
    scal_ref[2:8] = jnp.zeros((6, 128), F32)

    for b in range(BLOCKS):
        zac[b].wait_recv()
        for plane in range(2):
            for g in range(12):
                n_ref[plane, 8 * g : 8 * g + 4, 128 * b : 128 * (b + 1)] = nbuf[b, plane, 2 * g]
                n_ref[plane, 8 * g + 4 : 8 * g + 8, 128 * b : 128 * (b + 1)] = nbuf[b, plane, 2 * g + 1]
    for copy in started:
        copy.wait_send()


def on_device(tables, rows_n, groups_n, ys_n, solution, residual, direction, sens, sample_cell, kern, density):
    dma = pltpu.SemaphoreType.DMA
    vmem = pltpu.VMEM
    eight = (rows_n, 2)
    scratch = [
        vmem((192, 768), BF16), vmem((192, 768), BF16),
        vmem((rows_n, 384, EXT), BF16), vmem((rows_n, 384, EXT), BF16),
        vmem((rows_n, 16, SAMP), F32),
        vmem((rows_n, 2 * EXT, SAMP), BF16),
        vmem((rows_n, 2, BAND, SAMP), F32),
        vmem((384, SAMP), F32),
        vmem((4, BAND, 128), F32),
        vmem((384, SAMP), BF16), vmem((384, SAMP), BF16),
        vmem((rows_n, 2, 192, EXT), BF16), vmem((rows_n, 2, 192, EXT), BF16),
        vmem((rows_n, 2, 8, 128), F32), vmem((rows_n, 2, 8, 128), F32),
        vmem((rows_n, 2, 16, 128), F32),
        vmem((BLOCKS, 2, 24, 4, 128), F32),
        vmem((BLOCKS, 24, 4, 128), F32),
        vmem((BLOCKS, ys_n, 3, 4, 128), F32),
        vmem((BLOCKS, 24, 4, 128), F32),
        vmem((BLOCKS, 2, 24, 4, 128), F32),
        vmem((BLOCKS, 2, 24, 4, 128), F32),
        vmem((groups_n, 8, 128), F32), vmem((2, 8, 128), F32), vmem((ys_n, 8, 128), F32),
        vmem((rows_n, 2, 8, 128), F32),
        vmem((groups_n, 8, 128), F32), vmem((2, 8, 128), F32), vmem((ys_n, 8, 128), F32),
    ]
    one = (groups_n,), (groups_n,), (), (), (ys_n,), (ys_n,)
    for shape in (
        ((rows_n,), (rows_n,), eight, eight, eight, eight) + one + (eight, eight) + one
        + ((BLOCKS,), (BLOCKS,)) + ((BLOCKS, ys_n),) * 4 + ((BLOCKS,), (BLOCKS,))
    ):
        scratch.append(dma(shape) if shape else dma)
    spec = pl.BlockSpec(memory_space=pltpu.VMEM)
    normal, scal = pl.pallas_call(
        functools.partial(kernel, rows_n, groups_n, ys_n),
        out_shape=(
            jax.ShapeDtypeStruct((2, BAND, NXY), F32),
            jax.ShapeDtypeStruct((8, 128), F32),
        ),
        in_specs=[spec] * 10,
        out_specs=(spec, spec),
        scratch_shapes=scratch,
        compiler_params=pltpu.CompilerParams(
            collective_id=0, has_side_effects=True, vmem_limit_bytes=48 * 1024 * 1024
        ),
    )(
        direction[:, 0], residual[:, 0], sens[:, :, 0],
        sample_cell.reshape(1, SAMP), kern, density.reshape(4, 128), *tables,
    )
    step, ratio = scal[0, 0], scal[1, 0]
    normal = normal[:, None]
    solution_next = solution + step * direction
    residual_next = residual - step * normal
    direction_next = residual_next + ratio * direction
    return solution_next, residual_next, direction_next


def solution(mesh):
    rows_n = mesh.shape["row"]
    groups_n = mesh.shape["slab"] // 2
    ys_n = mesh.shape["coil"] // 2
    tables = transform_tables(rows_n)

    def whole(*args):
        return on_device([jnp.asarray(t) for t in tables], rows_n, groups_n, ys_n, *args)

    image = P(None, "slab", "row", None)
    return jax.shard_map(
        whole,
        mesh=mesh,
        in_specs=(
            image, image, image, P(None, "coil", "slab", "row", None),
            P("row"), P(None, None, "row"), P("row"),
        ),
        out_specs=(image, image, image),
        check_vma=False,
    )
```

```python
import functools
import math

import jax
import jax.numpy as jnp
import ml_dtypes
import numpy as np
from jax import lax
from jax.experimental import pallas as pl
from jax.experimental.pallas import tpu as pltpu
from jax.sharding import PartitionSpec as P

damping = 0.05
NXY = 384
BAND = 96
EXT = 128
HALO = 2
SAMP = 512
TAPS = 5
BLOCKS = 3
F32 = jnp.float32
BF16 = jnp.bfloat16
MESH = pl.DeviceIdType.MESH


def split_table(table):
    high = table.astype(np.float32).astype(ml_dtypes.bfloat16)
    low = (table - high.astype(np.float64)).astype(np.float32).astype(ml_dtypes.bfloat16)
    return high, low


def transform_tables(bands):
    x = np.arange(NXY)
    forward = np.zeros((bands, 2 * NXY, 2 * EXT))
    inverse = np.zeros((BLOCKS, bands * 2 * EXT, 256))
    scale = 1.0 / math.sqrt(NXY)
    for band in range(bands):
        k = (band * BAND - HALO + np.arange(EXT)) % NXY
        angle = (x[:, None] * k[None, :] % NXY) * (2.0 * math.pi / NXY)
        cosine, sine = np.cos(angle) * scale, np.sin(angle) * scale
        forward[band] = np.block([[cosine, -sine], [sine, cosine]])
        back = np.block([[cosine.T, sine.T], [-sine.T, cosine.T]])
        rows = slice(band * 2 * EXT, (band + 1) * 2 * EXT)
        for block in range(BLOCKS):
            cols = slice(block * 128, (block + 1) * 128)
            inverse[block, rows, :128] = back[:, :NXY][:, cols]
            inverse[block, rows, 128:] = back[:, NXY:][:, cols]
    return split_table(forward) + split_table(inverse)


def halves(value):
    high = value.astype(BF16)
    return high, (value - high.astype(F32)).astype(BF16)


def fold_phase(index):
    turn = index - NXY * jnp.floor(index * (1.0 / NXY) + 0.5)
    size = jnp.abs(turn)

    def sine_quarter(u):
        t = u * (2.0 * math.pi / NXY)
        q = t * t
        p = 1.0 / 6227020800.0
        for c in (-1.0 / 39916800.0, 1.0 / 362880.0, -1.0 / 5040.0, 1.0 / 120.0, -1.0 / 6.0, 1.0):
            p = p * q + c
        return p * t

    quarter = NXY // 4
    cosine = sine_quarter(quarter - size)
    sine = sine_quarter(quarter - jnp.abs(size - quarter))
    return cosine, jnp.where(turn < 0.0, -sine, sine)


def dot(a, b):
    return lax.dot_general(a, b, (((1,), (0,)), ((), ())), preferred_element_type=F32)


def dot_nt(a, b):
    return lax.dot_general(a, b, (((1,), (1,)), ((), ())), preferred_element_type=F32)


def kernel(
    rows_n, groups_n, ys_n,
    dir_in, res_in, sol_in, sens_in, cell_in, kern_in, dens_in,
    fh_in, fl_in, bh_in, bl_in,
    sol_out, res_out, dir_out,
    dir_ref, res_ref, sol_ref, sens_ref, cell_ref, dens_ref,
    fh_ref, fl_ref, bh_ref, bl_ref, in_sem,
    sol_buf, res_buf, dir_buf, out_sem,
    lhs_h, lhs_l, ke_h, ke_l, sinfo, cw, wr, tbuf, yconst, a_h, a_l, s_h, s_l,
    vsend, vrecv, wall, tz, zrecv, ysum, yrecv, nb, g1, e2, g2, y2,
    info_s, info_r, val_s, val_r, wt_s, wt_r, g1_s, g1_r, zr_s, zr_r, yr_s, yr_r,
    e2_s, e2_r, ya_s, ya_r, za_s, za_r, g2_s, g2_r, y2_s, y2_r,
):
    slab = lax.axis_index("slab")
    coil = lax.axis_index("coil")
    row = lax.axis_index("row")
    pair = slab // groups_n
    group = slab % groups_n
    zl = coil // ys_n
    yy = coil % ys_n
    half = SAMP // 128
    coils = 2 * ys_n
    orders = [0, 1, rows_n - 1] + list(range(2, rows_n - 1))
    ins = [
        pltpu.make_async_copy(src, dst, in_sem.at[i])
        for i, (src, dst) in enumerate((
            (cell_in, cell_ref), (kern_in, sinfo.at[row, pl.ds(0, 8 * TAPS)]), (dir_in, dir_ref), (sens_in, sens_ref),
            (fh_in, fh_ref), (fl_in, fl_ref), (res_in, res_ref), (dens_in, dens_ref),
            (sol_in, sol_ref), (bh_in, bh_ref), (bl_in, bl_ref),
        ))
    ]
    for copy in ins[:9]:
        copy.start()

    def remote(src, dst, send, recv, slab_to=None, coil_to=None, row_to=None):
        target = (
            slab if slab_to is None else slab_to,
            coil if coil_to is None else coil_to,
            row if row_to is None else row_to,
        )
        copy = pltpu.make_async_remote_copy(
            src_ref=src, dst_ref=dst, send_sem=send, recv_sem=recv,
            device_id=target, device_id_type=MESH,
        )
        copy.start()
        started.append(copy)
        return copy

    started = []

    def drain():
        for copy in started:
            copy.wait_send()
        started.clear()

    eight = [(k, e) for k in range(rows_n) for e in range(2) if (k, e) != (0, 0)]

    def eight_to(k, e):
        return (group + groups_n * ((pair + e) % 2), (row + k) % rows_n)

    barrier = pltpu.get_barrier_semaphore()
    count = 0
    for k, e in eight:
        s, r = eight_to(k, e)
        pl.semaphore_signal(barrier, inc=1, device_id=(s, coil, r), device_id_type=MESH)
        count += 1
    across = [(k, e) for k in range(groups_n) for e in range(2) if (k, e) != (0, 0)]

    def across_to(k, e):
        return (group + k) % groups_n + groups_n * pair, ((zl + e) % 2) * ys_n + yy

    for k, e in across:
        s, c = across_to(k, e)
        pl.semaphore_signal(barrier, inc=1, device_id=(s, c, row), device_id_type=MESH)
        count += 1

    def along_y(k):
        return zl * ys_n + (yy + k) % ys_n

    for k in range(1, ys_n):
        pl.semaphore_signal(barrier, inc=1, device_id=(slab, along_y(k), row), device_id_type=MESH)
        count += 1
    near = sorted(range(1, ys_n), key=lambda k: min(k, ys_n - k))

    first = (row * BAND).astype(F32)
    ypos = lax.broadcasted_iota(jnp.int32, (BAND, 128), 0).astype(F32) + first
    c1, s1 = fold_phase(ypos)
    yconst[0] = c1
    yconst[1] = s1
    yconst[2] = 2.0 * c1 * c1 - 1.0
    yconst[3] = 2.0 * s1 * c1

    ins[0].wait()
    ins[1].wait()
    sinfo[row, 8 * TAPS : 8 * TAPS + 4] = cell_ref[...].astype(F32)

    pl.semaphore_wait(barrier, count)
    info = [None] + [
        remote(sinfo.at[row], sinfo.at[row], info_s.at[k], info_r.at[k], row_to=(row + k) % rows_n)
        for k in range(1, rows_n)
    ]

    def wide(tile):
        return jnp.concatenate([tile] * half, axis=1)

    def tables(k):
        band = (row + k) % rows_n
        cell = jnp.concatenate([sinfo[band, 8 * TAPS + b : 8 * TAPS + b + 1] for b in range(half)], axis=1)
        kxs = jnp.floor((cell + 0.5) * (1.0 / NXY))
        ky = cell - NXY * kxs
        k0, k1 = [
            [
                jnp.concatenate(
                    [sinfo[band, 8 * t + 2 * b + q : 8 * t + 2 * b + q + 1] for b in range(half)], axis=1
                )
                for t in range(TAPS)
            ]
            for q in range(2)
        ]
        cells = lax.broadcasted_iota(jnp.int32, (16, SAMP), 0).astype(F32)
        for g in range(8):
            if g < 7:
                offset = cells + (16.0 * g) - kxs
                weight = jnp.where(offset == 4.0, k1[4], 0.0)
                for t in range(3, -1, -1):
                    weight = jnp.where(offset == float(t), k1[t], weight)
                high, low = halves(weight)
            else:
                high = low = jnp.zeros((16, SAMP), BF16)
            cw[k, 16 * g : 16 * g + 16] = high
            cw[k, EXT + 16 * g : EXT + 16 * g + 16] = low
        low_pos = lax.broadcasted_iota(jnp.int32, (8, SAMP), 0).astype(F32)
        lo_c, lo_s = fold_phase(low_pos * ky)
        lo_c = lo_c * (1.0 / math.sqrt(NXY))
        lo_s = lo_s * (1.0 / math.sqrt(NXY))
        high_pos = lax.broadcasted_iota(jnp.int32, (16, SAMP), 0).astype(F32) * 8.0 + first
        hi_c, hi_s = fold_phase(high_pos * ky)
        even1, odd1 = k0[3] + k0[1], k0[3] - k0[1]
        even2, odd2 = k0[4] + k0[0], k0[4] - k0[0]
        for p in range(BAND // 8):
            r8 = slice(8 * p, 8 * p + 8)
            pr = k0[2] + even1 * wide(yconst[0, r8]) + even2 * wide(yconst[2, r8])
            pi = odd1 * wide(yconst[1, r8]) + odd2 * wide(yconst[3, r8])
            hc, hs = hi_c[p : p + 1], hi_s[p : p + 1]
            er = hc * lo_c - hs * lo_s
            es = hs * lo_c + hc * lo_s
            wr[k, 0, r8] = er * pr - es * pi
            wr[k, 1, r8] = er * pi + es * pr

    tables(0)

    ins[2].wait()
    ins[3].wait()
    for c in range(2):
        sr, si = sens_ref[0, c].astype(F32), sens_ref[1, c].astype(F32)
        dr, di = dir_ref[0], dir_ref[1]
        re_h, re_l = halves(sr * dr - si * di)
        im_h, im_l = halves(sr * di + si * dr)
        here = slice(c * BAND, (c + 1) * BAND)
        lhs_h[here, 0:NXY] = re_h
        lhs_h[here, NXY:] = im_h
        lhs_l[here, 0:NXY] = re_l
        lhs_l[here, NXY:] = im_l

    ins[4].wait()
    ins[5].wait()
    for copy in ins[9:]:
        copy.start()
    for band in range(rows_n):
        out = dot(lhs_h[...], fh_ref[band])
        out = out + dot(lhs_l[...], fh_ref[band])
        out = out + dot(lhs_h[...], fl_ref[band])
        high, low = halves(out)
        ke_h[band, 0:192] = high[:, :EXT]
        ke_h[band, 192:384] = high[:, EXT:]
        ke_l[band, 0:192] = low[:, :EXT]
        ke_l[band, 192:384] = low[:, EXT:]

    vals = {}
    for k in orders:
        band = (row + k) % rows_n
        if k:
            info[rows_n - k].wait_recv()
            tables(k)
        kh, kl = ke_h[band], ke_l[band]
        tbuf[...] = dot(jnp.concatenate([kh, kh], axis=1), cw[k]) + dot(kl, cw[k, 0:EXT])
        for c in range(2):
            vr = jnp.zeros((8, SAMP), F32)
            vi = jnp.zeros((8, SAMP), F32)
            for p in range(BAND // 8):
                tr = tbuf[c * BAND + 8 * p : c * BAND + 8 * p + 8]
                ti = tbuf[192 + c * BAND + 8 * p : 192 + c * BAND + 8 * p + 8]
                w_r, w_i = wr[k, 0, 8 * p : 8 * p + 8], wr[k, 1, 8 * p : 8 * p + 8]
                vr = vr + w_r * tr + w_i * ti
                vi = vi + w_r * ti - w_i * tr
            vr = jnp.sum(vr, axis=0, keepdims=True)
            vi = jnp.sum(vi, axis=0, keepdims=True)
            for b in range(half):
                vsend[k, c, b : b + 1] = vr[:, 128 * b : 128 * (b + 1)]
                vsend[k, c, half + b : half + b + 1] = vi[:, 128 * b : 128 * (b + 1)]
        for e in range(2):
            if (k, e) == (0, 0):
                continue
            c = (pair + e) % 2
            s, r = eight_to(k, e)
            vals[k, e] = remote(
                vsend.at[k, c], vrecv.at[k, e], val_s.at[k, e], val_r.at[k, e], slab_to=s, row_to=r
            )

    total = vsend[0, pair]
    for k, e in eight:
        vals[k, e].wait_recv()
        total = total + vrecv[k, e]
    value = 0.5 * total
    ins[7].wait()
    dens = dens_ref[...]
    weighted = value * jnp.concatenate([dens, dens], axis=0)
    wall[row, pair, 0:8] = weighted
    curv = jnp.sum(weighted * value, axis=0, keepdims=True) * 2.0

    def lanes(tile):
        folded = tile[:, 0:128] + tile[:, 128:256] + tile[:, 256:384]
        return jnp.sum(folded, axis=0, keepdims=True)

    dd = lanes(dir_ref[0] * dir_ref[0] + dir_ref[1] * dir_ref[1])
    ins[6].wait()
    rr = lanes(res_ref[0] * res_ref[0] + res_ref[1] * res_ref[1])
    wall[row, pair, 8:9] = curv + dd * (damping / coils)
    wall[row, pair, 9:10] = rr * (1.0 / coils)
    wall[row, pair, 10:16] = jnp.zeros((6, 128), F32)
    wts = {}
    for k, e in eight:
        s, r = eight_to(k, e)
        wts[k, e] = remote(
            wall.at[row, pair], wall.at[row, pair], wt_s.at[k, e], wt_r.at[k, e], slab_to=s, row_to=r
        )

    for k in orders:
        band = (row + k) % rows_n
        for e in range(2):
            if (k, e) != (0, 0):
                wts[(rows_n - k) % rows_n, e].wait_recv()
        for c in range(2):
            w_re = jnp.concatenate([wall[band, c, b : b + 1] for b in range(half)], axis=1)
            w_im = jnp.concatenate([wall[band, c, half + b : half + b + 1] for b in range(half)], axis=1)
            for p in range(BAND // 16):
                m_r = wr[k, 0, 16 * p : 16 * p + 16]
                m_i = wr[k, 1, 16 * p : 16 * p + 16]
                re_h, re_l = halves(m_r * w_re - m_i * w_im)
                im_h, im_l = halves(m_r * w_im + m_i * w_re)
                here = slice(c * BAND + 16 * p, c * BAND + 16 * p + 16)
                there = slice(192 + c * BAND + 16 * p, 192 + c * BAND + 16 * p + 16)
                a_h[here] = re_h
                a_h[there] = im_h
                a_l[here] = re_l
                a_l[there] = im_l
        both = dot_nt(a_h[...], cw[k])
        out = both[:, :EXT] + both[:, EXT:] + dot_nt(a_l[...], cw[k, 0:EXT])
        high, low = halves(out)
        s_h[band, 0] = high[0:192]
        s_h[band, 1] = high[192:384]
        s_l[band, 0] = low[0:192]
        s_l[band, 1] = low[192:384]

    mine = jnp.zeros((8, 128), F32)
    for r in range(rows_n):
        for c in range(2):
            mine = mine + wall[r, c, 8:16]

    def to_across(buf, send, recv):
        copies = []
        for k, e in across:
            s, c = across_to(k, e)
            copies.append(
                remote(buf.at[group, zl], buf.at[group, zl], send.at[k, e], recv.at[k, e], slab_to=s, coil_to=c)
            )
        return copies

    def total_of(buf, first, second):
        mine = jnp.zeros((8, 128), F32)
        for i in range(first):
            for j in range(second):
                mine = mine + buf[i, j]
        return mine

    g1[group, zl] = mine
    g1c = to_across(g1, g1_s, g1_r)

    left_h = jnp.concatenate([s_h[j, q] for j in range(rows_n) for q in range(2)], axis=1)
    left_l = jnp.concatenate([s_l[j, q] for j in range(rows_n) for q in range(2)], axis=1)
    other = (1 - zl) * ys_n + yy
    zrc = []
    ins[9].wait()
    ins[10].wait()
    for b in range(BLOCKS):
        out = dot(left_h, bh_ref[b]) + dot(left_l, bh_ref[b]) + dot(left_h, bl_ref[b])
        cols = slice(128 * b, 128 * (b + 1))
        term_r = dir_ref[0, :, cols] * (damping / coils)
        term_i = dir_ref[1, :, cols] * (damping / coils)
        for c in range(2):
            sr = sens_ref[0, c, :, cols].astype(F32)
            si = sens_ref[1, c, :, cols].astype(F32)
            br = out[c * BAND : (c + 1) * BAND, :128]
            bi = out[c * BAND : (c + 1) * BAND, 128:]
            term_r = term_r + sr * br + si * bi
            term_i = term_i + sr * bi - si * br
        for g in range(24):
            tz[b, 0, g] = term_r[4 * g : 4 * g + 4]
            tz[b, 1, g] = term_i[4 * g : 4 * g + 4]
        zrc.append(remote(tz.at[b, 1 - zl], zrecv.at[b], zr_s.at[b], zr_r.at[b], coil_to=other))
    for copy in g1c:
        copy.wait_recv()
    mine = total_of(g1, groups_n, 2)
    for i in range(ys_n):
        ysum[i, 36:40] = mine[0:4]
    for b in range(BLOCKS):
        zrc[b].wait_recv()
        for i in range(ys_n):
            for g in range(3):
                at = 12 * b + 4 * g
                ysum[i, at : at + 4] = tz[b, zl, 3 * i + g] + zrecv[b, 3 * i + g]
    yrc = []
    for k in reversed(near):
        to = (yy + k) % ys_n
        yrc.append(remote(ysum.at[to], yrecv.at[yy], yr_s.at[k], yr_r.at[k], coil_to=along_y(k)))
    yrecv[yy] = ysum[yy]
    drain()
    for copy in yrc:
        copy.wait_recv()
    piece = yrecv[0]
    for c in range(1, ys_n):
        piece = piece + yrecv[c]
    curvature = jnp.sum(piece[36:37], axis=1, keepdims=True)
    norm_now = jnp.sum(piece[37:38], axis=1, keepdims=True)
    step = norm_now / curvature

    left = jnp.zeros((12, 128), F32)
    for b in range(BLOCKS):
        rows = res_ref[zl, pl.ds(pl.multiple_of(8 * (12 * yy // 8), 8), 16), 128 * b : 128 * (b + 1)]
        own = jnp.where(yy % 2 == 1, rows[4:16], rows[0:12])
        gap = own - step * piece[12 * b : 12 * b + 12]
        left = left + gap * gap
    nb[coil, 0:36] = piece[0:36]
    nb[coil, 36:40] = jnp.zeros((4, 128), F32)
    left = jnp.concatenate([left[0:4] + left[4:8] + left[8:12], jnp.zeros((4, 128), F32)], axis=0)
    e2[row, pair] = left
    e2c = []
    for k, e in eight:
        s, r = eight_to(k, e)
        e2c.append(
            remote(e2.at[row, pair], e2.at[row, pair], e2_s.at[k, e], e2_r.at[k, e], slab_to=s, row_to=r)
        )
    yac = {
        k: remote(nb.at[coil], nb.at[coil], ya_s.at[k], ya_r.at[k], coil_to=along_y(k)) for k in near
    }

    def forward(k):
        part = nb.at[zl * ys_n + (yy - k + ys_n) % ys_n]
        return remote(part, part, za_s.at[k], za_r.at[k], coil_to=other)

    zac = [forward(0)]
    ins[8].wait()
    sol_buf[...] = sol_ref[...] + step * dir_ref[...]
    outs = [
        pltpu.make_async_copy(src, dst, out_sem.at[i])
        for i, (src, dst) in enumerate(((sol_buf, sol_out), (res_buf, res_out), (dir_buf, dir_out)))
    ]
    outs[0].start()
    for copy in e2c:
        copy.wait_recv()
    g2[group, zl] = total_of(e2, rows_n, 2)
    g2c = to_across(g2, g2_s, g2_r)
    for k in near:
        yac[k].wait_recv()
        zac.append(forward(k))
    for copy in g2c:
        copy.wait_recv()
    y2[yy] = total_of(g2, groups_n, 2)
    y2c = [
        remote(y2.at[yy], y2.at[yy], y2_s.at[k], y2_r.at[k], coil_to=along_y(k)) for k in range(1, ys_n)
    ]
    for copy in zac:
        copy.wait_recv()
    for b in range(BLOCKS):
        cols = slice(128 * b, 128 * (b + 1))
        for plane in range(2):
            for g in range(12):
                here = slice(8 * g, 8 * g + 8)
                parts = []
                for u in (2 * g, 2 * g + 1):
                    at = 12 * b + 4 * (u % 3)
                    parts.append(nb[plane * ys_n + u // 3, at : at + 4])
                normal = jnp.concatenate(parts, axis=0)
                res_buf[plane, here, cols] = res_ref[plane, here, cols] - step * normal
    outs[1].start()
    for copy in y2c:
        copy.wait_recv()
    mine = y2[0]
    for c in range(1, ys_n):
        mine = mine + y2[c]
    folded = jnp.sum(mine[0:4], axis=0, keepdims=True)
    ratio = jnp.sum(folded, axis=1, keepdims=True) / norm_now
    dir_buf[...] = res_buf[...] + ratio * dir_ref[...]
    outs[2].start()
    drain()
    for copy in outs:
        copy.wait()


def put_kernel(a_ref, b_ref, c_ref, a_out, b_out, c_out, a_buf, b_buf, c_buf, load_sems, store_sems):
    refs = ((a_ref, a_buf, a_out), (b_ref, b_buf, b_out), (c_ref, c_buf, c_out))
    loads = [pltpu.make_async_copy(src, buf, load_sems.at[i]) for i, (src, buf, _) in enumerate(refs)]
    stores = [pltpu.make_async_copy(buf, dst, store_sems.at[i]) for i, (_, buf, dst) in enumerate(refs)]
    for copy in loads:
        copy.start()
    for load, store in zip(loads, stores):
        load.wait()
        store.start()
    for copy in stores:
        copy.wait()


def on_device(tables, rows_n, groups_n, ys_n, solution, residual, direction, sens, sample_cell, kern, density):
    dma = pltpu.SemaphoreType.DMA
    vmem = pltpu.VMEM
    eight = (rows_n, 2)
    image = (2, BAND, NXY)
    scratch = [
        vmem(image, F32), vmem(image, F32), vmem(image, F32), vmem((2,) + image, BF16),
        vmem((4, 128), jnp.int32), vmem((4, 128), F32),
        vmem(tables[0].shape, BF16), vmem(tables[1].shape, BF16),
        vmem(tables[2].shape, BF16), vmem(tables[3].shape, BF16), dma((11,)),
        vmem(image, F32), vmem(image, F32), vmem(image, F32), dma((3,)),
        vmem((192, 768), BF16), vmem((192, 768), BF16),
        vmem((rows_n, 384, EXT), BF16), vmem((rows_n, 384, EXT), BF16),
        vmem((rows_n, 48, 128), F32),
        vmem((rows_n, 2 * EXT, SAMP), BF16),
        vmem((rows_n, 2, BAND, SAMP), F32),
        vmem((384, SAMP), F32),
        vmem((4, BAND, 128), F32),
        vmem((384, SAMP), BF16), vmem((384, SAMP), BF16),
        vmem((rows_n, 2, 192, EXT), BF16), vmem((rows_n, 2, 192, EXT), BF16),
        vmem((rows_n, 2, 8, 128), F32), vmem((rows_n, 2, 8, 128), F32),
        vmem((rows_n, 2, 16, 128), F32),
        vmem((BLOCKS, 2, 24, 4, 128), F32), vmem((BLOCKS, 24, 4, 128), F32),
        vmem((ys_n, 40, 128), F32), vmem((ys_n, 40, 128), F32), vmem((2 * ys_n, 40, 128), F32),
        vmem((groups_n, 2, 8, 128), F32), vmem((rows_n, 2, 8, 128), F32),
        vmem((groups_n, 2, 8, 128), F32), vmem((ys_n, 8, 128), F32),
    ]
    few, cross, ys, blocks = (rows_n,), (groups_n, 2), (ys_n,), (BLOCKS,)
    for shape in (few, eight, eight, cross, blocks, ys, eight, ys, ys, cross, ys):
        scratch.append(dma(shape))
        scratch.append(dma(shape))
    far = pl.BlockSpec(memory_space=pl.ANY)
    shapes = (jax.ShapeDtypeStruct(image, F32),) * 3
    taps = kern.reshape(2, TAPS, 4, 128).transpose(1, 2, 0, 3).reshape(8 * TAPS, 128)
    outs = pl.pallas_call(
        functools.partial(kernel, rows_n, groups_n, ys_n),
        out_shape=shapes,
        in_specs=[far] * 11,
        out_specs=(far,) * 3,
        scratch_shapes=scratch,
        compiler_params=pltpu.CompilerParams(
            collective_id=0, has_side_effects=True, vmem_limit_bytes=56000 * 1024
        ),
    )(
        direction[:, 0], residual[:, 0], solution[:, 0], sens[:, :, 0],
        sample_cell.reshape(4, 128), taps, density.reshape(4, 128), *tables,
    )
    outs = pl.pallas_call(
        put_kernel,
        out_shape=shapes,
        in_specs=[far] * 3,
        out_specs=(far,) * 3,
        scratch_shapes=[vmem(image, F32)] * 3 + [dma((3,))] * 2, compiler_params=pltpu.CompilerParams(vmem_limit_bytes=56000 * 1024),
    )(*outs)
    return tuple(out[:, None] for out in outs)


def solution(mesh):
    rows_n = mesh.shape["row"]
    groups_n = mesh.shape["slab"] // 2
    ys_n = mesh.shape["coil"] // 2
    tables = transform_tables(rows_n)

    def whole(*args):
        return on_device([jnp.asarray(t) for t in tables], rows_n, groups_n, ys_n, *args)

    image = P(None, "slab", "row", None)
    return jax.shard_map(
        whole,
        mesh=mesh,
        in_specs=(
            image, image, image, P(None, "coil", "slab", "row", None),
            P("row"), P(None, None, "row"), P("row"),
        ),
        out_specs=(image, image, image),
        check_vma=False,
    )
```

```python
import functools
import math

import jax
import jax.numpy as jnp
import ml_dtypes
import numpy as np
from jax import lax
from jax.experimental import pallas as pl
from jax.experimental.pallas import tpu as pltpu
from jax.sharding import PartitionSpec as P

damping = 0.05
NXY = 384
BAND = 96
EXT = 128
HALO = 2
SAMP = 512
TAPS = 5
BLOCKS = 3
F32 = jnp.float32
BF16 = jnp.bfloat16
MESH = pl.DeviceIdType.MESH


def split_table(table):
    high = table.astype(np.float32).astype(ml_dtypes.bfloat16)
    low = (table - high.astype(np.float64)).astype(np.float32).astype(ml_dtypes.bfloat16)
    return high, low


def transform_tables(bands):
    x = np.arange(NXY)
    forward = np.zeros((bands, 2 * NXY, 2 * EXT))
    inverse = np.zeros((BLOCKS, bands * 2 * EXT, 256))
    scale = 1.0 / math.sqrt(NXY)
    for band in range(bands):
        k = (band * BAND - HALO + np.arange(EXT)) % NXY
        angle = (x[:, None] * k[None, :] % NXY) * (2.0 * math.pi / NXY)
        cosine, sine = np.cos(angle) * scale, np.sin(angle) * scale
        forward[band] = np.block([[cosine, -sine], [sine, cosine]])
        back = np.block([[cosine.T, sine.T], [-sine.T, cosine.T]])
        rows = slice(band * 2 * EXT, (band + 1) * 2 * EXT)
        for block in range(BLOCKS):
            cols = slice(block * 128, (block + 1) * 128)
            inverse[block, rows, :128] = back[:, :NXY][:, cols]
            inverse[block, rows, 128:] = back[:, NXY:][:, cols]
    return split_table(forward) + split_table(inverse)


def halves(value):
    high = value.astype(BF16)
    return high, (value - high.astype(F32)).astype(BF16)


def fold_phase(index):
    turn = index - NXY * jnp.floor(index * (1.0 / NXY) + 0.5)
    size = jnp.abs(turn)

    def sine_quarter(u):
        t = u * (2.0 * math.pi / NXY)
        q = t * t
        p = 1.0 / 6227020800.0
        for c in (-1.0 / 39916800.0, 1.0 / 362880.0, -1.0 / 5040.0, 1.0 / 120.0, -1.0 / 6.0, 1.0):
            p = p * q + c
        return p * t

    quarter = NXY // 4
    cosine = sine_quarter(quarter - size)
    sine = sine_quarter(quarter - jnp.abs(size - quarter))
    return cosine, jnp.where(turn < 0.0, -sine, sine)


def dot(a, b):
    return lax.dot_general(a, b, (((1,), (0,)), ((), ())), preferred_element_type=F32)


def dot_nt(a, b):
    return lax.dot_general(a, b, (((1,), (1,)), ((), ())), preferred_element_type=F32)


def kernel(
    rows_n, groups_n, ys_n,
    dir_in, res_in, sol_in, sens_in, cell_in, kern_in, dens_in,
    fh_in, fl_in, bh_in, bl_in,
    sol_out, res_out, dir_out,
    dir_ref, res_ref, sol_ref, sens_ref, cell_ref, dens_ref,
    fh_ref, fl_ref, bh_ref, bl_ref, in_sem,
    sol_buf, res_buf, dir_buf, out_sem,
    lhs_h, lhs_l, ke_h, ke_l, sinfo, cw, wr, tbuf, yconst, a_h, a_l, s_h, s_l,
    vall, wall, scs, tz, zrecv, ysum, yrecv, nb, g1, e2, g2, y2,
    info_s, info_r, val_s, val_r, sc_s, sc_r, g1_s, g1_r, zr_s, zr_r, yr_s, yr_r,
    e2_s, e2_r, ya_s, ya_r, za_s, za_r, g2_s, g2_r, y2_s, y2_r,
):
    slab = lax.axis_index("slab")
    coil = lax.axis_index("coil")
    row = lax.axis_index("row")
    pair = slab // groups_n
    group = slab % groups_n
    zl = coil // ys_n
    yy = coil % ys_n
    half = SAMP // 128
    coils = 2 * ys_n
    orders = [0, 1, rows_n - 1] + list(range(2, rows_n - 1))
    ins = [
        pltpu.make_async_copy(src, dst, in_sem.at[i])
        for i, (src, dst) in enumerate((
            (cell_in, cell_ref), (kern_in, sinfo.at[row, pl.ds(0, 8 * TAPS)]), (dir_in, dir_ref), (sens_in, sens_ref),
            (fh_in, fh_ref), (fl_in, fl_ref), (res_in, res_ref), (dens_in, dens_ref),
            (sol_in, sol_ref), (bh_in, bh_ref), (bl_in, bl_ref),
        ))
    ]
    for i in (0, 1, 7, 2, 3, 4, 5, 6, 8):
        ins[i].start()

    def remote(src, dst, send, recv, slab_to=None, coil_to=None, row_to=None):
        target = (
            slab if slab_to is None else slab_to,
            coil if coil_to is None else coil_to,
            row if row_to is None else row_to,
        )
        copy = pltpu.make_async_remote_copy(
            src_ref=src, dst_ref=dst, send_sem=send, recv_sem=recv,
            device_id=target, device_id_type=MESH,
        )
        copy.start()
        started.append(copy)
        return copy

    started = []

    def drain():
        for copy in started:
            copy.wait_send()
        started.clear()

    eight = [(k, e) for k in range(rows_n) for e in range(2) if (k, e) != (0, 0)]

    def eight_to(k, e):
        return (group + groups_n * ((pair + e) % 2), (row + k) % rows_n)

    barrier = pltpu.get_barrier_semaphore()
    count = 0
    for k, e in eight:
        s, r = eight_to(k, e)
        pl.semaphore_signal(barrier, inc=1, device_id=(s, coil, r), device_id_type=MESH)
        count += 1
    across = [(k, e) for k in range(groups_n) for e in range(2) if (k, e) != (0, 0)]

    def across_to(k, e):
        return (group + k) % groups_n + groups_n * pair, ((zl + e) % 2) * ys_n + yy

    for k, e in across:
        s, c = across_to(k, e)
        pl.semaphore_signal(barrier, inc=1, device_id=(s, c, row), device_id_type=MESH)
        count += 1

    def along_y(k):
        return zl * ys_n + (yy + k) % ys_n

    for k in range(1, ys_n):
        pl.semaphore_signal(barrier, inc=1, device_id=(slab, along_y(k), row), device_id_type=MESH)
        count += 1
    near = sorted(range(1, ys_n), key=lambda k: min(k, ys_n - k))

    first = (row * BAND).astype(F32)
    ypos = lax.broadcasted_iota(jnp.int32, (BAND, 128), 0).astype(F32) + first
    c1, s1 = fold_phase(ypos)
    yconst[0] = c1
    yconst[1] = s1
    yconst[2] = 2.0 * c1 * c1 - 1.0
    yconst[3] = 2.0 * s1 * c1

    ins[0].wait()
    ins[1].wait()
    sinfo[row, 8 * TAPS : 8 * TAPS + 4] = cell_ref[...].astype(F32)
    ins[7].wait()
    sinfo[row, 8 * TAPS + 4 : 8 * TAPS + 8] = dens_ref[...]

    pl.semaphore_wait(barrier, count)
    info = [None] + [
        remote(sinfo.at[row], sinfo.at[row], info_s.at[k], info_r.at[k], row_to=(row + k) % rows_n)
        for k in range(1, rows_n)
    ]

    def wide(tile):
        return jnp.concatenate([tile] * half, axis=1)

    def tables(k):
        band = (row + k) % rows_n
        cell = jnp.concatenate([sinfo[band, 8 * TAPS + b : 8 * TAPS + b + 1] for b in range(half)], axis=1)
        kxs = jnp.floor((cell + 0.5) * (1.0 / NXY))
        ky = cell - NXY * kxs
        k0, k1 = [
            [
                jnp.concatenate(
                    [sinfo[band, 8 * t + 2 * b + q : 8 * t + 2 * b + q + 1] for b in range(half)], axis=1
                )
                for t in range(TAPS)
            ]
            for q in range(2)
        ]
        cells = lax.broadcasted_iota(jnp.int32, (16, SAMP), 0).astype(F32)
        for g in range(8):
            if g < 7:
                offset = cells + (16.0 * g) - kxs
                weight = jnp.where(offset == 4.0, k1[4], 0.0)
                for t in range(3, -1, -1):
                    weight = jnp.where(offset == float(t), k1[t], weight)
                high, low = halves(weight)
            else:
                high = low = jnp.zeros((16, SAMP), BF16)
            cw[k, 16 * g : 16 * g + 16] = high
            cw[k, EXT + 16 * g : EXT + 16 * g + 16] = low
        low_pos = lax.broadcasted_iota(jnp.int32, (8, SAMP), 0).astype(F32)
        lo_c, lo_s = fold_phase(low_pos * ky)
        lo_c = lo_c * (1.0 / math.sqrt(NXY))
        lo_s = lo_s * (1.0 / math.sqrt(NXY))
        high_pos = lax.broadcasted_iota(jnp.int32, (16, SAMP), 0).astype(F32) * 8.0 + first
        hi_c, hi_s = fold_phase(high_pos * ky)
        even1, odd1 = k0[3] + k0[1], k0[3] - k0[1]
        even2, odd2 = k0[4] + k0[0], k0[4] - k0[0]
        for p in range(BAND // 8):
            r8 = slice(8 * p, 8 * p + 8)
            pr = k0[2] + even1 * wide(yconst[0, r8]) + even2 * wide(yconst[2, r8])
            pi = odd1 * wide(yconst[1, r8]) + odd2 * wide(yconst[3, r8])
            hc, hs = hi_c[p : p + 1], hi_s[p : p + 1]
            er = hc * lo_c - hs * lo_s
            es = hs * lo_c + hc * lo_s
            wr[k, 0, r8] = er * pr - es * pi
            wr[k, 1, r8] = er * pi + es * pr

    tables(0)

    ins[2].wait()
    ins[3].wait()
    for c in range(2):
        sr, si = sens_ref[0, c].astype(F32), sens_ref[1, c].astype(F32)
        dr, di = dir_ref[0], dir_ref[1]
        re_h, re_l = halves(sr * dr - si * di)
        im_h, im_l = halves(sr * di + si * dr)
        here = slice(c * BAND, (c + 1) * BAND)
        lhs_h[here, 0:NXY] = re_h
        lhs_h[here, NXY:] = im_h
        lhs_l[here, 0:NXY] = re_l
        lhs_l[here, NXY:] = im_l

    ins[4].wait()
    ins[5].wait()
    for copy in ins[9:]:
        copy.start()
    for band in range(rows_n):
        out = dot(lhs_h[...], fh_ref[band])
        out = out + dot(lhs_l[...], fh_ref[band])
        out = out + dot(lhs_h[...], fl_ref[band])
        high, low = halves(out)
        ke_h[band, 0:192] = high[:, :EXT]
        ke_h[band, 192:384] = high[:, EXT:]
        ke_l[band, 0:192] = low[:, :EXT]
        ke_l[band, 192:384] = low[:, EXT:]

    def lanes(tile):
        folded = tile[:, 0:128] + tile[:, 128:256] + tile[:, 256:384]
        return jnp.sum(folded, axis=0, keepdims=True)

    ins[6].wait()
    dd = lanes(dir_ref[0] * dir_ref[0] + dir_ref[1] * dir_ref[1])
    rr = lanes(res_ref[0] * res_ref[0] + res_ref[1] * res_ref[1])
    scs[row, pair] = jnp.concatenate(
        [dd * (damping / coils), rr * (1.0 / coils), jnp.zeros((6, 128), F32)], axis=0
    )
    scc = []
    for k, e in eight:
        s, r = eight_to(k, e)
        scc.append(
            remote(scs.at[row, pair], scs.at[row, pair], sc_s.at[k, e], sc_r.at[k, e], slab_to=s, row_to=r)
        )

    vals = {}
    for k in orders:
        band = (row + k) % rows_n
        if k:
            info[rows_n - k].wait_recv()
            tables(k)
        kh, kl = ke_h[band], ke_l[band]
        tbuf[...] = dot(jnp.concatenate([kh, kh], axis=1), cw[k]) + dot(kl, cw[k, 0:EXT])
        for c in range(2):
            vr = jnp.zeros((8, SAMP), F32)
            vi = jnp.zeros((8, SAMP), F32)
            for p in range(BAND // 8):
                tr = tbuf[c * BAND + 8 * p : c * BAND + 8 * p + 8]
                ti = tbuf[192 + c * BAND + 8 * p : 192 + c * BAND + 8 * p + 8]
                w_r, w_i = wr[k, 0, 8 * p : 8 * p + 8], wr[k, 1, 8 * p : 8 * p + 8]
                vr = vr + w_r * tr + w_i * ti
                vi = vi + w_r * ti - w_i * tr
            vr = jnp.sum(vr, axis=0, keepdims=True)
            vi = jnp.sum(vi, axis=0, keepdims=True)
            for b in range(half):
                vall[row, pair, band, c, b : b + 1] = vr[:, 128 * b : 128 * (b + 1)]
                vall[row, pair, band, c, half + b : half + b + 1] = vi[:, 128 * b : 128 * (b + 1)]
        for tk, e in eight:
            s, r = eight_to(tk, e)
            part = vall.at[row, pair, band]
            vals[k, tk, e] = remote(part, part, val_s.at[k, tk, e], val_r.at[k, tk, e], slab_to=s, row_to=r)

    power = jnp.zeros((8, 128), F32)
    for k in orders:
        band = (row + k) % rows_n
        for tk, e in eight:
            vals[(k + tk) % rows_n, tk, e].wait_recv()
        total = jnp.zeros((2, 8, 128), F32)
        for r in range(rows_n):
            for p in range(2):
                total = total + vall[r, p, band]
        value = 0.5 * total
        dens = sinfo[band, 8 * TAPS + 4 : 8 * TAPS + 8]
        weighted = value * jnp.concatenate([dens, dens], axis=0)[None]
        wall[band] = weighted
        power = power + weighted[0] * value[0] + weighted[1] * value[1]
        for c in range(2):
            w_re = jnp.concatenate([wall[band, c, b : b + 1] for b in range(half)], axis=1)
            w_im = jnp.concatenate([wall[band, c, half + b : half + b + 1] for b in range(half)], axis=1)
            for p in range(BAND // 16):
                m_r = wr[k, 0, 16 * p : 16 * p + 16]
                m_i = wr[k, 1, 16 * p : 16 * p + 16]
                re_h, re_l = halves(m_r * w_re - m_i * w_im)
                im_h, im_l = halves(m_r * w_im + m_i * w_re)
                here = slice(c * BAND + 16 * p, c * BAND + 16 * p + 16)
                there = slice(192 + c * BAND + 16 * p, 192 + c * BAND + 16 * p + 16)
                a_h[here] = re_h
                a_h[there] = im_h
                a_l[here] = re_l
                a_l[there] = im_l
        both = dot_nt(a_h[...], cw[k])
        out = both[:, :EXT] + both[:, EXT:] + dot_nt(a_l[...], cw[k, 0:EXT])
        high, low = halves(out)
        s_h[band, 0] = high[0:192]
        s_h[band, 1] = high[192:384]
        s_l[band, 0] = low[0:192]
        s_l[band, 1] = low[192:384]

    for copy in scc:
        copy.wait_recv()
    mine = jnp.zeros((8, 128), F32)
    for r in range(rows_n):
        for c in range(2):
            mine = mine + scs[r, c]
    curv = 2.0 * jnp.sum(power, axis=0, keepdims=True)
    mine = mine + jnp.concatenate([curv, jnp.zeros((7, 128), F32)], axis=0)

    def to_across(buf, send, recv):
        copies = []
        for k, e in across:
            s, c = across_to(k, e)
            copies.append(
                remote(buf.at[group, zl], buf.at[group, zl], send.at[k, e], recv.at[k, e], slab_to=s, coil_to=c)
            )
        return copies

    def total_of(buf, first, second):
        mine = jnp.zeros((8, 128), F32)
        for i in range(first):
            for j in range(second):
                mine = mine + buf[i, j]
        return mine

    g1[group, zl] = mine
    g1c = to_across(g1, g1_s, g1_r)

    left_h = jnp.concatenate([s_h[j, q] for j in range(rows_n) for q in range(2)], axis=1)
    left_l = jnp.concatenate([s_l[j, q] for j in range(rows_n) for q in range(2)], axis=1)
    other = (1 - zl) * ys_n + yy
    zrc = []
    ins[9].wait()
    ins[10].wait()
    for b in range(BLOCKS):
        out = dot(left_h, bh_ref[b]) + dot(left_l, bh_ref[b]) + dot(left_h, bl_ref[b])
        cols = slice(128 * b, 128 * (b + 1))
        term_r = dir_ref[0, :, cols] * (damping / coils)
        term_i = dir_ref[1, :, cols] * (damping / coils)
        for c in range(2):
            sr = sens_ref[0, c, :, cols].astype(F32)
            si = sens_ref[1, c, :, cols].astype(F32)
            br = out[c * BAND : (c + 1) * BAND, :128]
            bi = out[c * BAND : (c + 1) * BAND, 128:]
            term_r = term_r + sr * br + si * bi
            term_i = term_i + sr * bi - si * br
        for g in range(24):
            tz[b, 0, g] = term_r[4 * g : 4 * g + 4]
            tz[b, 1, g] = term_i[4 * g : 4 * g + 4]
        zrc.append(remote(tz.at[b, 1 - zl], zrecv.at[b], zr_s.at[b], zr_r.at[b], coil_to=other))
    for copy in g1c:
        copy.wait_recv()
    mine = total_of(g1, groups_n, 2)
    for i in range(ys_n):
        ysum[i, 36:40] = mine[0:4]
    for b in range(BLOCKS):
        zrc[b].wait_recv()
        for i in range(ys_n):
            for g in range(3):
                at = 12 * b + 4 * g
                ysum[i, at : at + 4] = tz[b, zl, 3 * i + g] + zrecv[b, 3 * i + g]
    yrc = []
    for k in reversed(near):
        to = (yy + k) % ys_n
        yrc.append(remote(ysum.at[to], yrecv.at[yy], yr_s.at[k], yr_r.at[k], coil_to=along_y(k)))
    yrecv[yy] = ysum[yy]
    drain()
    for copy in yrc:
        copy.wait_recv()
    piece = yrecv[0]
    for c in range(1, ys_n):
        piece = piece + yrecv[c]
    curvature = jnp.sum(piece[36:37], axis=1, keepdims=True)
    norm_now = jnp.sum(piece[37:38], axis=1, keepdims=True)
    step = norm_now / curvature

    left = jnp.zeros((12, 128), F32)
    for b in range(BLOCKS):
        rows = res_ref[zl, pl.ds(pl.multiple_of(8 * (12 * yy // 8), 8), 16), 128 * b : 128 * (b + 1)]
        own = jnp.where(yy % 2 == 1, rows[4:16], rows[0:12])
        gap = own - step * piece[12 * b : 12 * b + 12]
        left = left + gap * gap
    nb[coil, 0:36] = piece[0:36]
    nb[coil, 36:40] = jnp.zeros((4, 128), F32)
    left = jnp.concatenate([left[0:4] + left[4:8] + left[8:12], jnp.zeros((4, 128), F32)], axis=0)
    e2[row, pair] = left
    e2c = []
    for k, e in eight:
        s, r = eight_to(k, e)
        e2c.append(
            remote(e2.at[row, pair], e2.at[row, pair], e2_s.at[k, e], e2_r.at[k, e], slab_to=s, row_to=r)
        )
    yac = {
        k: remote(nb.at[coil], nb.at[coil], ya_s.at[k], ya_r.at[k], coil_to=along_y(k)) for k in near
    }

    def forward(k):
        part = nb.at[zl * ys_n + (yy - k + ys_n) % ys_n]
        return remote(part, part, za_s.at[k], za_r.at[k], coil_to=other)

    zac = [forward(0)]
    ins[8].wait()
    sol_buf[...] = sol_ref[...] + step * dir_ref[...]
    outs = [
        pltpu.make_async_copy(src, dst, out_sem.at[i])
        for i, (src, dst) in enumerate(((sol_buf, sol_out), (res_buf, res_out), (dir_buf, dir_out)))
    ]
    outs[0].start()
    for copy in e2c:
        copy.wait_recv()
    g2[group, zl] = total_of(e2, rows_n, 2)
    g2c = to_across(g2, g2_s, g2_r)
    for k in near:
        yac[k].wait_recv()
        zac.append(forward(k))
    for copy in g2c:
        copy.wait_recv()
    y2[yy] = total_of(g2, groups_n, 2)
    y2c = [
        remote(y2.at[yy], y2.at[yy], y2_s.at[k], y2_r.at[k], coil_to=along_y(k)) for k in range(1, ys_n)
    ]
    for copy in zac:
        copy.wait_recv()
    for b in range(BLOCKS):
        cols = slice(128 * b, 128 * (b + 1))
        for plane in range(2):
            for g in range(12):
                here = slice(8 * g, 8 * g + 8)
                parts = []
                for u in (2 * g, 2 * g + 1):
                    at = 12 * b + 4 * (u % 3)
                    parts.append(nb[plane * ys_n + u // 3, at : at + 4])
                normal = jnp.concatenate(parts, axis=0)
                res_buf[plane, here, cols] = res_ref[plane, here, cols] - step * normal
    outs[1].start()
    for copy in y2c:
        copy.wait_recv()
    mine = y2[0]
    for c in range(1, ys_n):
        mine = mine + y2[c]
    folded = jnp.sum(mine[0:4], axis=0, keepdims=True)
    ratio = jnp.sum(folded, axis=1, keepdims=True) / norm_now
    dir_buf[...] = res_buf[...] + ratio * dir_ref[...]
    outs[2].start()
    drain()
    for copy in outs:
        copy.wait()


def put_kernel(a_ref, b_ref, c_ref, a_out, b_out, c_out, a_buf, b_buf, c_buf, load_sems, store_sems):
    refs = ((a_ref, a_buf, a_out), (b_ref, b_buf, b_out), (c_ref, c_buf, c_out))
    loads = [pltpu.make_async_copy(src, buf, load_sems.at[i]) for i, (src, buf, _) in enumerate(refs)]
    stores = [pltpu.make_async_copy(buf, dst, store_sems.at[i]) for i, (_, buf, dst) in enumerate(refs)]
    for copy in loads:
        copy.start()
    for load, store in zip(loads, stores):
        load.wait()
        store.start()
    for copy in stores:
        copy.wait()


def on_device(tables, rows_n, groups_n, ys_n, solution, residual, direction, sens, sample_cell, kern, density):
    dma = pltpu.SemaphoreType.DMA
    vmem = pltpu.VMEM
    eight = (rows_n, 2)
    image = (2, BAND, NXY)
    scratch = [
        vmem(image, F32), vmem(image, F32), vmem(image, F32), vmem((2,) + image, BF16),
        vmem((4, 128), jnp.int32), vmem((4, 128), F32),
        vmem(tables[0].shape, BF16), vmem(tables[1].shape, BF16),
        vmem(tables[2].shape, BF16), vmem(tables[3].shape, BF16), dma((11,)),
        vmem(image, F32), vmem(image, F32), vmem(image, F32), dma((3,)),
        vmem((192, 768), BF16), vmem((192, 768), BF16),
        vmem((rows_n, 384, EXT), BF16), vmem((rows_n, 384, EXT), BF16),
        vmem((rows_n, 48, 128), F32),
        vmem((rows_n, 2 * EXT, SAMP), BF16),
        vmem((rows_n, 2, BAND, SAMP), F32),
        vmem((384, SAMP), F32),
        vmem((4, BAND, 128), F32),
        vmem((384, SAMP), BF16), vmem((384, SAMP), BF16),
        vmem((rows_n, 2, 192, EXT), BF16), vmem((rows_n, 2, 192, EXT), BF16),
        vmem((rows_n, 2, rows_n, 2, 8, 128), F32), vmem((rows_n, 2, 8, 128), F32),
        vmem((rows_n, 2, 8, 128), F32),
        vmem((BLOCKS, 2, 24, 4, 128), F32), vmem((BLOCKS, 24, 4, 128), F32),
        vmem((ys_n, 40, 128), F32), vmem((ys_n, 40, 128), F32), vmem((2 * ys_n, 40, 128), F32),
        vmem((groups_n, 2, 8, 128), F32), vmem((rows_n, 2, 8, 128), F32),
        vmem((groups_n, 2, 8, 128), F32), vmem((ys_n, 8, 128), F32),
    ]
    few, cross, ys, blocks = (rows_n,), (groups_n, 2), (ys_n,), (BLOCKS,)
    for shape in (few, (rows_n,) + eight, eight, cross, blocks, ys, eight, ys, ys, cross, ys):
        scratch.append(dma(shape))
        scratch.append(dma(shape))
    far = pl.BlockSpec(memory_space=pl.ANY)
    shapes = (jax.ShapeDtypeStruct(image, F32),) * 3
    taps = kern.reshape(2, TAPS, 4, 128).transpose(1, 2, 0, 3).reshape(8 * TAPS, 128)
    outs = pl.pallas_call(
        functools.partial(kernel, rows_n, groups_n, ys_n),
        out_shape=shapes,
        in_specs=[far] * 11,
        out_specs=(far,) * 3,
        scratch_shapes=scratch,
        compiler_params=pltpu.CompilerParams(
            collective_id=0, has_side_effects=True, vmem_limit_bytes=56000 * 1024
        ),
    )(
        direction[:, 0], residual[:, 0], solution[:, 0], sens[:, :, 0],
        sample_cell.reshape(4, 128), taps, density.reshape(4, 128), *tables,
    )
    outs = pl.pallas_call(
        put_kernel,
        out_shape=shapes,
        in_specs=[far] * 3,
        out_specs=(far,) * 3,
        scratch_shapes=[vmem(image, F32)] * 3 + [dma((3,))] * 2, compiler_params=pltpu.CompilerParams(vmem_limit_bytes=56000 * 1024),
    )(*outs)
    return tuple(out[:, None] for out in outs)


def solution(mesh):
    rows_n = mesh.shape["row"]
    groups_n = mesh.shape["slab"] // 2
    ys_n = mesh.shape["coil"] // 2
    tables = transform_tables(rows_n)

    def whole(*args):
        return on_device([jnp.asarray(t) for t in tables], rows_n, groups_n, ys_n, *args)

    image = P(None, "slab", "row", None)
    return jax.shard_map(
        whole,
        mesh=mesh,
        in_specs=(
            image, image, image, P(None, "coil", "slab", "row", None),
            P("row"), P(None, None, "row"), P("row"),
        ),
        out_specs=(image, image, image),
        check_vma=False,
    )
```

```python
import functools
import math

import jax
import jax.numpy as jnp
import ml_dtypes
import numpy as np
from jax import lax
from jax.experimental import pallas as pl
from jax.experimental.pallas import tpu as pltpu
from jax.sharding import PartitionSpec as P

damping = 0.05
NXY = 384
BAND = 96
EXT = 128
HALO = 2
SAMP = 512
TAPS = 5
BLOCKS = 3
F32 = jnp.float32
BF16 = jnp.bfloat16
MESH = pl.DeviceIdType.MESH


def split_table(table):
    high = table.astype(np.float32).astype(ml_dtypes.bfloat16)
    low = (table - high.astype(np.float64)).astype(np.float32).astype(ml_dtypes.bfloat16)
    return high, low


def transform_tables(bands):
    x = np.arange(NXY)
    forward = np.zeros((bands, 2 * NXY, 2 * EXT))
    inverse = np.zeros((BLOCKS, bands * 2 * EXT, 256))
    scale = 1.0 / math.sqrt(NXY)
    for band in range(bands):
        k = (band * BAND - HALO + np.arange(EXT)) % NXY
        angle = (x[:, None] * k[None, :] % NXY) * (2.0 * math.pi / NXY)
        cosine, sine = np.cos(angle) * scale, np.sin(angle) * scale
        forward[band] = np.block([[cosine, -sine], [sine, cosine]])
        back = np.block([[cosine.T, sine.T], [-sine.T, cosine.T]])
        rows = slice(band * 2 * EXT, (band + 1) * 2 * EXT)
        for block in range(BLOCKS):
            cols = slice(block * 128, (block + 1) * 128)
            inverse[block, rows, :128] = back[:, :NXY][:, cols]
            inverse[block, rows, 128:] = back[:, NXY:][:, cols]
    return split_table(forward) + split_table(inverse)


def halves(value):
    high = value.astype(BF16)
    return high, (value - high.astype(F32)).astype(BF16)


def fold_phase(index):
    turn = index - NXY * jnp.floor(index * (1.0 / NXY) + 0.5)
    size = jnp.abs(turn)

    def sine_quarter(u):
        t = u * (2.0 * math.pi / NXY)
        q = t * t
        p = 1.0 / 6227020800.0
        for c in (-1.0 / 39916800.0, 1.0 / 362880.0, -1.0 / 5040.0, 1.0 / 120.0, -1.0 / 6.0, 1.0):
            p = p * q + c
        return p * t

    quarter = NXY // 4
    cosine = sine_quarter(quarter - size)
    sine = sine_quarter(quarter - jnp.abs(size - quarter))
    return cosine, jnp.where(turn < 0.0, -sine, sine)


def dot(a, b):
    return lax.dot_general(a, b, (((1,), (0,)), ((), ())), preferred_element_type=F32)


def dot_nt(a, b):
    return lax.dot_general(a, b, (((1,), (1,)), ((), ())), preferred_element_type=F32)


def kernel(
    rows_n, groups_n, ys_n,
    dir_in, res_in, sol_in, sens_in, cell_in, kern_in, dens_in,
    fh_in, fl_in, bh_in, bl_in,
    sol_out, res_out, dir_out,
    dir_ref, res_ref, sol_ref, sens_ref, cell_ref, dens_ref,
    fh_ref, fl_ref, bh_ref, bl_ref, in_sem,
    sol_buf, res_buf, dir_buf, out_sem,
    lhs_h, lhs_l, ke_h, ke_l, sinfo, cw, wr, tbuf, yconst, a_h, a_l, s_h, s_l,
    vall, wall, scs, tz, zrecv, ysum, yrecv, nb, g1, e2, c2,
    info_s, info_r, val_s, val_r, sc_s, sc_r, g1_s, g1_r, zr_s, zr_r, yr_s, yr_r,
    e2_s, e2_r, ya_s, ya_r, za_s, za_r, c2_s, c2_r,
):
    slab = lax.axis_index("slab")
    coil = lax.axis_index("coil")
    row = lax.axis_index("row")
    pair = slab // groups_n
    group = slab % groups_n
    zl = coil // ys_n
    yy = coil % ys_n
    half = SAMP // 128
    coils = 2 * ys_n
    orders = [0, 1, rows_n - 1] + list(range(2, rows_n - 1))
    ins = [
        pltpu.make_async_copy(src, dst, in_sem.at[i])
        for i, (src, dst) in enumerate((
            (cell_in, cell_ref), (kern_in, sinfo.at[row, pl.ds(0, 8 * TAPS)]), (dir_in, dir_ref), (sens_in, sens_ref),
            (fh_in, fh_ref), (fl_in, fl_ref), (res_in, res_ref), (dens_in, dens_ref),
            (sol_in, sol_ref), (bh_in, bh_ref), (bl_in, bl_ref),
        ))
    ]
    for i in (0, 1, 7, 2, 3, 4, 5, 6, 8):
        ins[i].start()

    def remote(src, dst, send, recv, slab_to=None, coil_to=None, row_to=None):
        target = (
            slab if slab_to is None else slab_to,
            coil if coil_to is None else coil_to,
            row if row_to is None else row_to,
        )
        copy = pltpu.make_async_remote_copy(
            src_ref=src, dst_ref=dst, send_sem=send, recv_sem=recv,
            device_id=target, device_id_type=MESH,
        )
        copy.start()
        started.append(copy)
        return copy

    started = []

    def drain():
        for copy in started:
            copy.wait_send()
        started.clear()

    eight = [(k, e) for k in range(rows_n) for e in range(2) if (k, e) != (0, 0)]

    def eight_to(k, e):
        return (group + groups_n * ((pair + e) % 2), (row + k) % rows_n)

    barrier = pltpu.get_barrier_semaphore()
    count = 0
    slabs = 2 * groups_n

    def hops(d, dr):
        return min(d, slabs - d) + 4 * min(dr, rows_n - dr)

    wide_set = sorted(
        ((d, dr) for d in range(slabs) for dr in range(rows_n) if (d, dr) != (0, 0)),
        key=lambda t: -hops(*t),
    )
    for d, dr in wide_set:
        pl.semaphore_signal(
            barrier, inc=1, device_id=((slab + d) % slabs, coil, (row + dr) % rows_n), device_id_type=MESH
        )
        count += 1
    across = [(k, e) for k in range(groups_n) for e in range(2) if (k, e) != (0, 0)]

    def across_to(k, e):
        return (group + k) % groups_n + groups_n * pair, ((zl + e) % 2) * ys_n + yy

    for k, e in across:
        if k == 0 or e == 0:
            continue
        s, c = across_to(k, e)
        pl.semaphore_signal(barrier, inc=1, device_id=(s, c, row), device_id_type=MESH)
        count += 1

    def along_y(k):
        return zl * ys_n + (yy + k) % ys_n

    coil_set = sorted(range(1, coils), key=lambda k: -min(k % ys_n, ys_n - k % ys_n))
    for k in coil_set:
        pl.semaphore_signal(
            barrier, inc=1, device_id=(slab, (coil + k) % coils, row), device_id_type=MESH
        )
        count += 1
    near = sorted(range(1, ys_n), key=lambda k: min(k, ys_n - k))

    first = (row * BAND).astype(F32)
    ypos = lax.broadcasted_iota(jnp.int32, (BAND, 128), 0).astype(F32) + first
    c1, s1 = fold_phase(ypos)
    yconst[0] = c1
    yconst[1] = s1
    yconst[2] = 2.0 * c1 * c1 - 1.0
    yconst[3] = 2.0 * s1 * c1

    ins[0].wait()
    ins[1].wait()
    sinfo[row, 8 * TAPS : 8 * TAPS + 4] = cell_ref[...].astype(F32)
    ins[7].wait()
    sinfo[row, 8 * TAPS + 4 : 8 * TAPS + 8] = dens_ref[...]

    pl.semaphore_wait(barrier, count)
    info = [None] + [
        remote(sinfo.at[row], sinfo.at[row], info_s.at[k], info_r.at[k], row_to=(row + k) % rows_n)
        for k in range(1, rows_n)
    ]

    def wide(tile):
        return jnp.concatenate([tile] * half, axis=1)

    def tables(k):
        band = (row + k) % rows_n
        cell = jnp.concatenate([sinfo[band, 8 * TAPS + b : 8 * TAPS + b + 1] for b in range(half)], axis=1)
        kxs = jnp.floor((cell + 0.5) * (1.0 / NXY))
        ky = cell - NXY * kxs
        k0, k1 = [
            [
                jnp.concatenate(
                    [sinfo[band, 8 * t + 2 * b + q : 8 * t + 2 * b + q + 1] for b in range(half)], axis=1
                )
                for t in range(TAPS)
            ]
            for q in range(2)
        ]
        cells = lax.broadcasted_iota(jnp.int32, (16, SAMP), 0).astype(F32)
        for g in range(8):
            if g < 7:
                offset = cells + (16.0 * g) - kxs
                weight = jnp.where(offset == 4.0, k1[4], 0.0)
                for t in range(3, -1, -1):
                    weight = jnp.where(offset == float(t), k1[t], weight)
                high, low = halves(weight)
            else:
                high = low = jnp.zeros((16, SAMP), BF16)
            cw[k, 16 * g : 16 * g + 16] = high
            cw[k, EXT + 16 * g : EXT + 16 * g + 16] = low
        low_pos = lax.broadcasted_iota(jnp.int32, (8, SAMP), 0).astype(F32)
        lo_c, lo_s = fold_phase(low_pos * ky)
        lo_c = lo_c * (1.0 / math.sqrt(NXY))
        lo_s = lo_s * (1.0 / math.sqrt(NXY))
        high_pos = lax.broadcasted_iota(jnp.int32, (16, SAMP), 0).astype(F32) * 8.0 + first
        hi_c, hi_s = fold_phase(high_pos * ky)
        even1, odd1 = k0[3] + k0[1], k0[3] - k0[1]
        even2, odd2 = k0[4] + k0[0], k0[4] - k0[0]
        for p in range(BAND // 8):
            r8 = slice(8 * p, 8 * p + 8)
            pr = k0[2] + even1 * wide(yconst[0, r8]) + even2 * wide(yconst[2, r8])
            pi = odd1 * wide(yconst[1, r8]) + odd2 * wide(yconst[3, r8])
            hc, hs = hi_c[p : p + 1], hi_s[p : p + 1]
            er = hc * lo_c - hs * lo_s
            es = hs * lo_c + hc * lo_s
            wr[k, 0, r8] = er * pr - es * pi
            wr[k, 1, r8] = er * pi + es * pr

    tables(0)

    ins[2].wait()
    ins[3].wait()
    for c in range(2):
        sr, si = sens_ref[0, c].astype(F32), sens_ref[1, c].astype(F32)
        dr, di = dir_ref[0], dir_ref[1]
        re_h, re_l = halves(sr * dr - si * di)
        im_h, im_l = halves(sr * di + si * dr)
        here = slice(c * BAND, (c + 1) * BAND)
        lhs_h[here, 0:NXY] = re_h
        lhs_h[here, NXY:] = im_h
        lhs_l[here, 0:NXY] = re_l
        lhs_l[here, NXY:] = im_l

    ins[4].wait()
    ins[5].wait()
    for copy in ins[9:]:
        copy.start()
    for band in range(rows_n):
        out = dot(lhs_h[...], fh_ref[band])
        out = out + dot(lhs_l[...], fh_ref[band])
        out = out + dot(lhs_h[...], fl_ref[band])
        high, low = halves(out)
        ke_h[band, 0:192] = high[:, :EXT]
        ke_h[band, 192:384] = high[:, EXT:]
        ke_l[band, 0:192] = low[:, :EXT]
        ke_l[band, 192:384] = low[:, EXT:]

    def lanes(tile):
        folded = tile[:, 0:128] + tile[:, 128:256] + tile[:, 256:384]
        return jnp.sum(folded, axis=0, keepdims=True)

    ins[6].wait()
    dd = lanes(dir_ref[0] * dir_ref[0] + dir_ref[1] * dir_ref[1])
    rr = lanes(res_ref[0] * res_ref[0] + res_ref[1] * res_ref[1])
    scs[row, pair] = jnp.concatenate(
        [dd * (damping / coils), rr * (1.0 / coils), jnp.zeros((6, 128), F32)], axis=0
    )
    scc = []
    for k, e in eight:
        s, r = eight_to(k, e)
        scc.append(
            remote(scs.at[row, pair], scs.at[row, pair], sc_s.at[k, e], sc_r.at[k, e], slab_to=s, row_to=r)
        )

    vals = {}
    for k in orders:
        band = (row + k) % rows_n
        if k:
            info[rows_n - k].wait_recv()
            tables(k)
        kh, kl = ke_h[band], ke_l[band]
        tbuf[...] = dot(jnp.concatenate([kh, kh], axis=1), cw[k]) + dot(kl, cw[k, 0:EXT])
        for c in range(2):
            vr = jnp.zeros((8, SAMP), F32)
            vi = jnp.zeros((8, SAMP), F32)
            for p in range(BAND // 8):
                tr = tbuf[c * BAND + 8 * p : c * BAND + 8 * p + 8]
                ti = tbuf[192 + c * BAND + 8 * p : 192 + c * BAND + 8 * p + 8]
                w_r, w_i = wr[k, 0, 8 * p : 8 * p + 8], wr[k, 1, 8 * p : 8 * p + 8]
                vr = vr + w_r * tr + w_i * ti
                vi = vi + w_r * ti - w_i * tr
            vr = jnp.sum(vr, axis=0, keepdims=True)
            vi = jnp.sum(vi, axis=0, keepdims=True)
            for b in range(half):
                vall[row, pair, band, c, b : b + 1] = vr[:, 128 * b : 128 * (b + 1)]
                vall[row, pair, band, c, half + b : half + b + 1] = vi[:, 128 * b : 128 * (b + 1)]
        for tk, e in eight:
            s, r = eight_to(tk, e)
            part = vall.at[row, pair, band]
            vals[k, tk, e] = remote(part, part, val_s.at[k, tk, e], val_r.at[k, tk, e], slab_to=s, row_to=r)

    power = jnp.zeros((8, 128), F32)
    for k in orders:
        band = (row + k) % rows_n
        for tk, e in eight:
            vals[(k + tk) % rows_n, tk, e].wait_recv()
        total = jnp.zeros((2, 8, 128), F32)
        for r in range(rows_n):
            for p in range(2):
                total = total + vall[r, p, band]
        value = 0.5 * total
        dens = sinfo[band, 8 * TAPS + 4 : 8 * TAPS + 8]
        weighted = value * jnp.concatenate([dens, dens], axis=0)[None]
        wall[band] = weighted
        power = power + weighted[0] * value[0] + weighted[1] * value[1]
        for c in range(2):
            w_re = jnp.concatenate([wall[band, c, b : b + 1] for b in range(half)], axis=1)
            w_im = jnp.concatenate([wall[band, c, half + b : half + b + 1] for b in range(half)], axis=1)
            for p in range(BAND // 16):
                m_r = wr[k, 0, 16 * p : 16 * p + 16]
                m_i = wr[k, 1, 16 * p : 16 * p + 16]
                re_h, re_l = halves(m_r * w_re - m_i * w_im)
                im_h, im_l = halves(m_r * w_im + m_i * w_re)
                here = slice(c * BAND + 16 * p, c * BAND + 16 * p + 16)
                there = slice(192 + c * BAND + 16 * p, 192 + c * BAND + 16 * p + 16)
                a_h[here] = re_h
                a_h[there] = im_h
                a_l[here] = re_l
                a_l[there] = im_l
        both = dot_nt(a_h[...], cw[k])
        out = both[:, :EXT] + both[:, EXT:] + dot_nt(a_l[...], cw[k, 0:EXT])
        high, low = halves(out)
        s_h[band, 0] = high[0:192]
        s_h[band, 1] = high[192:384]
        s_l[band, 0] = low[0:192]
        s_l[band, 1] = low[192:384]

    for copy in scc:
        copy.wait_recv()
    mine = jnp.zeros((8, 128), F32)
    for r in range(rows_n):
        for c in range(2):
            mine = mine + scs[r, c]
    curv = 2.0 * jnp.sum(power, axis=0, keepdims=True)
    mine = mine + jnp.concatenate([curv, jnp.zeros((7, 128), F32)], axis=0)

    def to_across(buf, send, recv):
        copies = []
        for k, e in across:
            s, c = across_to(k, e)
            copies.append(
                remote(buf.at[group, zl], buf.at[group, zl], send.at[k, e], recv.at[k, e], slab_to=s, coil_to=c)
            )
        return copies

    def total_of(buf, first, second):
        mine = jnp.zeros((8, 128), F32)
        for i in range(first):
            for j in range(second):
                mine = mine + buf[i, j]
        return mine

    g1[group, zl] = mine
    g1c = to_across(g1, g1_s, g1_r)

    left_h = jnp.concatenate([s_h[j, q] for j in range(rows_n) for q in range(2)], axis=1)
    left_l = jnp.concatenate([s_l[j, q] for j in range(rows_n) for q in range(2)], axis=1)
    other = (1 - zl) * ys_n + yy
    zrc = []
    ins[9].wait()
    ins[10].wait()
    for b in range(BLOCKS):
        out = dot(left_h, bh_ref[b]) + dot(left_l, bh_ref[b]) + dot(left_h, bl_ref[b])
        cols = slice(128 * b, 128 * (b + 1))
        term_r = dir_ref[0, :, cols] * (damping / coils)
        term_i = dir_ref[1, :, cols] * (damping / coils)
        for c in range(2):
            sr = sens_ref[0, c, :, cols].astype(F32)
            si = sens_ref[1, c, :, cols].astype(F32)
            br = out[c * BAND : (c + 1) * BAND, :128]
            bi = out[c * BAND : (c + 1) * BAND, 128:]
            term_r = term_r + sr * br + si * bi
            term_i = term_i + sr * bi - si * br
        for g in range(24):
            tz[b, 0, g] = term_r[4 * g : 4 * g + 4]
            tz[b, 1, g] = term_i[4 * g : 4 * g + 4]
        zrc.append(remote(tz.at[b, 1 - zl], zrecv.at[b], zr_s.at[b], zr_r.at[b], coil_to=other))
    for copy in g1c:
        copy.wait_recv()
    mine = total_of(g1, groups_n, 2)
    for i in range(ys_n):
        ysum[i, 36:40] = mine[0:4]
    for b in range(BLOCKS):
        zrc[b].wait_recv()
        for i in range(ys_n):
            for g in range(3):
                at = 12 * b + 4 * g
                ysum[i, at : at + 4] = tz[b, zl, 3 * i + g] + zrecv[b, 3 * i + g]
    yrc = []
    for k in reversed(near):
        to = (yy + k) % ys_n
        yrc.append(remote(ysum.at[to], yrecv.at[yy], yr_s.at[k], yr_r.at[k], coil_to=along_y(k)))
    yrecv[yy] = ysum[yy]
    drain()
    for copy in yrc:
        copy.wait_recv()
    piece = yrecv[0]
    for c in range(1, ys_n):
        piece = piece + yrecv[c]
    curvature = jnp.sum(piece[36:37], axis=1, keepdims=True)
    norm_now = jnp.sum(piece[37:38], axis=1, keepdims=True)
    step = norm_now / curvature

    left = jnp.zeros((12, 128), F32)
    for b in range(BLOCKS):
        rows = res_ref[zl, pl.ds(pl.multiple_of(8 * (12 * yy // 8), 8), 16), 128 * b : 128 * (b + 1)]
        own = jnp.where(yy % 2 == 1, rows[4:16], rows[0:12])
        gap = own - step * piece[12 * b : 12 * b + 12]
        left = left + gap * gap
    nb[coil, 0:36] = piece[0:36]
    nb[coil, 36:40] = jnp.zeros((4, 128), F32)
    e2[slab, row] = jnp.sum(left, axis=0, keepdims=True)
    e2c = [
        remote(e2.at[slab, row], e2.at[slab, row], e2_s.at[d, dr], e2_r.at[d, dr],
               slab_to=(slab + d) % slabs, row_to=(row + dr) % rows_n)
        for d, dr in wide_set
    ]
    yac = {
        k: remote(nb.at[coil], nb.at[coil], ya_s.at[k], ya_r.at[k], coil_to=along_y(k)) for k in near
    }

    def forward(k):
        part = nb.at[zl * ys_n + (yy - k + ys_n) % ys_n]
        return remote(part, part, za_s.at[k], za_r.at[k], coil_to=other)

    zac = [forward(0)]
    ins[8].wait()
    sol_buf[...] = sol_ref[...] + step * dir_ref[...]
    outs = [
        pltpu.make_async_copy(src, dst, out_sem.at[i])
        for i, (src, dst) in enumerate(((sol_buf, sol_out), (res_buf, res_out), (dir_buf, dir_out)))
    ]
    outs[0].start()
    for copy in e2c:
        copy.wait_recv()
    mine = jnp.zeros((1, 128), F32)
    for i in range(slabs):
        for r in range(rows_n):
            mine = mine + e2[i, r]
    c2[coil] = mine
    c2c = [
        remote(c2.at[coil], c2.at[coil], c2_s.at[k], c2_r.at[k], coil_to=(coil + k) % coils)
        for k in coil_set
    ]
    for k in near:
        yac[k].wait_recv()
        zac.append(forward(k))
    for copy in zac:
        copy.wait_recv()
    for b in range(BLOCKS):
        cols = slice(128 * b, 128 * (b + 1))
        for plane in range(2):
            for g in range(12):
                here = slice(8 * g, 8 * g + 8)
                parts = []
                for u in (2 * g, 2 * g + 1):
                    at = 12 * b + 4 * (u % 3)
                    parts.append(nb[plane * ys_n + u // 3, at : at + 4])
                normal = jnp.concatenate(parts, axis=0)
                res_buf[plane, here, cols] = res_ref[plane, here, cols] - step * normal
    outs[1].start()
    for copy in c2c:
        copy.wait_recv()
    folded = c2[0]
    for c in range(1, coils):
        folded = folded + c2[c]
    ratio = jnp.sum(folded, axis=1, keepdims=True) / norm_now
    dir_buf[...] = res_buf[...] + ratio * dir_ref[...]
    outs[2].start()
    drain()
    for copy in outs:
        copy.wait()


def put_kernel(a_ref, b_ref, c_ref, a_out, b_out, c_out, a_buf, b_buf, c_buf, load_sems, store_sems):
    refs = ((a_ref, a_buf, a_out), (b_ref, b_buf, b_out), (c_ref, c_buf, c_out))
    loads = [pltpu.make_async_copy(src, buf, load_sems.at[i]) for i, (src, buf, _) in enumerate(refs)]
    stores = [pltpu.make_async_copy(buf, dst, store_sems.at[i]) for i, (_, buf, dst) in enumerate(refs)]
    for copy in loads:
        copy.start()
    for load, store in zip(loads, stores):
        load.wait()
        store.start()
    for copy in stores:
        copy.wait()


def on_device(tables, rows_n, groups_n, ys_n, solution, residual, direction, sens, sample_cell, kern, density):
    dma = pltpu.SemaphoreType.DMA
    vmem = pltpu.VMEM
    eight = (rows_n, 2)
    image = (2, BAND, NXY)
    scratch = [
        vmem(image, F32), vmem(image, F32), vmem(image, F32), vmem((2,) + image, BF16),
        vmem((4, 128), jnp.int32), vmem((4, 128), F32),
        vmem(tables[0].shape, BF16), vmem(tables[1].shape, BF16),
        vmem(tables[2].shape, BF16), vmem(tables[3].shape, BF16), dma((11,)),
        vmem(image, F32), vmem(image, F32), vmem(image, F32), dma((3,)),
        vmem((192, 768), BF16), vmem((192, 768), BF16),
        vmem((rows_n, 384, EXT), BF16), vmem((rows_n, 384, EXT), BF16),
        vmem((rows_n, 48, 128), F32),
        vmem((rows_n, 2 * EXT, SAMP), BF16),
        vmem((rows_n, 2, BAND, SAMP), F32),
        vmem((384, SAMP), F32),
        vmem((4, BAND, 128), F32),
        vmem((384, SAMP), BF16), vmem((384, SAMP), BF16),
        vmem((rows_n, 2, 192, EXT), BF16), vmem((rows_n, 2, 192, EXT), BF16),
        vmem((rows_n, 2, rows_n, 2, 8, 128), F32), vmem((rows_n, 2, 8, 128), F32),
        vmem((rows_n, 2, 8, 128), F32),
        vmem((BLOCKS, 2, 24, 4, 128), F32), vmem((BLOCKS, 24, 4, 128), F32),
        vmem((ys_n, 40, 128), F32), vmem((ys_n, 40, 128), F32), vmem((2 * ys_n, 40, 128), F32),
        vmem((groups_n, 2, 8, 128), F32),
        vmem((2 * groups_n, rows_n, 1, 128), F32), vmem((2 * ys_n, 1, 128), F32),
    ]
    few, cross, ys, blocks = (rows_n,), (groups_n, 2), (ys_n,), (BLOCKS,)
    for shape in (few, (rows_n,) + eight, eight, cross, blocks, ys, (2 * groups_n, rows_n), ys, ys, (2 * ys_n,)):
        scratch.append(dma(shape))
        scratch.append(dma(shape))
    far = pl.BlockSpec(memory_space=pl.ANY)
    shapes = (jax.ShapeDtypeStruct(image, F32),) * 3
    taps = kern.reshape(2, TAPS, 4, 128).transpose(1, 2, 0, 3).reshape(8 * TAPS, 128)
    outs = pl.pallas_call(
        functools.partial(kernel, rows_n, groups_n, ys_n),
        out_shape=shapes,
        in_specs=[far] * 11,
        out_specs=(far,) * 3,
        scratch_shapes=scratch,
        compiler_params=pltpu.CompilerParams(
            collective_id=0, has_side_effects=True, vmem_limit_bytes=56000 * 1024
        ),
    )(
        direction[:, 0], residual[:, 0], solution[:, 0], sens[:, :, 0],
        sample_cell.reshape(4, 128), taps, density.reshape(4, 128), *tables,
    )
    outs = pl.pallas_call(
        put_kernel,
        out_shape=shapes,
        in_specs=[far] * 3,
        out_specs=(far,) * 3,
        scratch_shapes=[vmem(image, F32)] * 3 + [dma((3,))] * 2, compiler_params=pltpu.CompilerParams(vmem_limit_bytes=56000 * 1024),
    )(*outs)
    return tuple(out[:, None] for out in outs)


def solution(mesh):
    rows_n = mesh.shape["row"]
    groups_n = mesh.shape["slab"] // 2
    ys_n = mesh.shape["coil"] // 2
    tables = transform_tables(rows_n)

    def whole(*args):
        return on_device([jnp.asarray(t) for t in tables], rows_n, groups_n, ys_n, *args)

    image = P(None, "slab", "row", None)
    return jax.shard_map(
        whole,
        mesh=mesh,
        in_specs=(
            image, image, image, P(None, "coil", "slab", "row", None),
            P("row"), P(None, None, "row"), P("row"),
        ),
        out_specs=(image, image, image),
        check_vma=False,
    )
```

```python
import functools
import math

import jax
import jax.numpy as jnp
import ml_dtypes
import numpy as np
from jax import lax
from jax.experimental import pallas as pl
from jax.experimental.pallas import tpu as pltpu
from jax.sharding import PartitionSpec as P

damping = 0.05
NXY = 384
BAND = 96
EXT = 128
HALO = 2
SAMP = 512
TAPS = 5
BLOCKS = 3
F32 = jnp.float32
BF16 = jnp.bfloat16
MESH = pl.DeviceIdType.MESH


def split_table(table):
    high = table.astype(np.float32).astype(ml_dtypes.bfloat16)
    low = (table - high.astype(np.float64)).astype(np.float32).astype(ml_dtypes.bfloat16)
    return high, low


def transform_tables(bands):
    x = np.arange(NXY)
    forward = np.zeros((bands, 2 * NXY, 2 * EXT))
    inverse = np.zeros((BLOCKS, bands * 2 * EXT, 256))
    scale = 1.0 / math.sqrt(NXY)
    for band in range(bands):
        k = (band * BAND - HALO + np.arange(EXT)) % NXY
        angle = (x[:, None] * k[None, :] % NXY) * (2.0 * math.pi / NXY)
        cosine, sine = np.cos(angle) * scale, np.sin(angle) * scale
        forward[band] = np.block([[cosine, -sine], [sine, cosine]])
        back = np.block([[cosine.T, sine.T], [-sine.T, cosine.T]])
        rows = slice(band * 2 * EXT, (band + 1) * 2 * EXT)
        for block in range(BLOCKS):
            cols = slice(block * 128, (block + 1) * 128)
            inverse[block, rows, :128] = back[:, :NXY][:, cols]
            inverse[block, rows, 128:] = back[:, NXY:][:, cols]
    return split_table(forward) + split_table(inverse)


def halves(value):
    high = value.astype(BF16)
    return high, (value - high.astype(F32)).astype(BF16)


def fold_phase(index):
    turn = index - NXY * jnp.floor(index * (1.0 / NXY) + 0.5)
    size = jnp.abs(turn)

    def sine_quarter(u):
        t = u * (2.0 * math.pi / NXY)
        q = t * t
        p = 1.0 / 6227020800.0
        for c in (-1.0 / 39916800.0, 1.0 / 362880.0, -1.0 / 5040.0, 1.0 / 120.0, -1.0 / 6.0, 1.0):
            p = p * q + c
        return p * t

    quarter = NXY // 4
    cosine = sine_quarter(quarter - size)
    sine = sine_quarter(quarter - jnp.abs(size - quarter))
    return cosine, jnp.where(turn < 0.0, -sine, sine)


def dot(a, b):
    return lax.dot_general(a, b, (((1,), (0,)), ((), ())), preferred_element_type=F32)


def dot_nt(a, b):
    return lax.dot_general(a, b, (((1,), (1,)), ((), ())), preferred_element_type=F32)


def kernel(
    rows_n, groups_n, ys_n,
    dir_in, res_in, sol_in, sens_in, cell_in, kern_in, dens_in,
    fh_in, fl_in, bh_in, bl_in,
    sol_out, res_out, ratio_out,
    dir_ref, res_ref, sol_ref, sens_ref, cell_ref, dens_ref,
    fh_ref, fl_ref, bh_ref, bl_ref, in_sem,
    sol_buf, res_buf, ratio_buf, out_sem,
    lhs_h, lhs_l, ke_h, ke_l, sinfo, cw, wr, tbuf, yconst, a_h, a_l, s_h, s_l,
    vall, wall, scs, tz, zrecv, ysum, yrecv, nb, g1, e2, c2,
    info_s, info_r, val_s, val_r, sc_s, sc_r, g1_s, g1_r, zr_s, zr_r, yr_s, yr_r,
    e2_s, e2_r, ya_s, ya_r, za_s, za_r, c2_s, c2_r,
):
    slab = lax.axis_index("slab")
    coil = lax.axis_index("coil")
    row = lax.axis_index("row")
    pair = slab // groups_n
    group = slab % groups_n
    zl = coil // ys_n
    yy = coil % ys_n
    half = SAMP // 128
    coils = 2 * ys_n
    orders = [0, 1, rows_n - 1] + list(range(2, rows_n - 1))
    ins = [
        pltpu.make_async_copy(src, dst, in_sem.at[i])
        for i, (src, dst) in enumerate((
            (cell_in, cell_ref), (kern_in, sinfo.at[row, pl.ds(0, 8 * TAPS)]), (dir_in, dir_ref), (sens_in, sens_ref),
            (fh_in, fh_ref), (fl_in, fl_ref), (res_in, res_ref), (dens_in, dens_ref),
            (sol_in, sol_ref), (bh_in, bh_ref), (bl_in, bl_ref),
        ))
    ]
    for i in (0, 1, 7, 2, 3, 4, 5, 6, 8):
        ins[i].start()

    def remote(src, dst, send, recv, slab_to=None, coil_to=None, row_to=None):
        target = (
            slab if slab_to is None else slab_to,
            coil if coil_to is None else coil_to,
            row if row_to is None else row_to,
        )
        copy = pltpu.make_async_remote_copy(
            src_ref=src, dst_ref=dst, send_sem=send, recv_sem=recv,
            device_id=target, device_id_type=MESH,
        )
        copy.start()
        started.append(copy)
        return copy

    started = []

    def drain():
        for copy in started:
            copy.wait_send()
        started.clear()

    eight = [(k, e) for k in range(rows_n) for e in range(2) if (k, e) != (0, 0)]

    def eight_to(k, e):
        return (group + groups_n * ((pair + e) % 2), (row + k) % rows_n)

    barrier = pltpu.get_barrier_semaphore()
    count = 0
    slabs = 2 * groups_n

    def hops(d, dr):
        return min(d, slabs - d) + 4 * min(dr, rows_n - dr)

    wide_set = sorted(
        ((d, dr) for d in range(slabs) for dr in range(rows_n) if (d, dr) != (0, 0)),
        key=lambda t: -hops(*t),
    )
    for d, dr in wide_set:
        pl.semaphore_signal(
            barrier, inc=1, device_id=((slab + d) % slabs, coil, (row + dr) % rows_n), device_id_type=MESH
        )
        count += 1
    across = [(k, e) for k in range(groups_n) for e in range(2) if (k, e) != (0, 0)]

    def across_to(k, e):
        return (group + k) % groups_n + groups_n * pair, ((zl + e) % 2) * ys_n + yy

    for k, e in across:
        if k == 0 or e == 0:
            continue
        s, c = across_to(k, e)
        pl.semaphore_signal(barrier, inc=1, device_id=(s, c, row), device_id_type=MESH)
        count += 1

    def along_y(k):
        return zl * ys_n + (yy + k) % ys_n

    coil_set = sorted(range(1, coils), key=lambda k: -min(k % ys_n, ys_n - k % ys_n))
    for k in coil_set:
        pl.semaphore_signal(
            barrier, inc=1, device_id=(slab, (coil + k) % coils, row), device_id_type=MESH
        )
        count += 1
    near = sorted(range(1, ys_n), key=lambda k: min(k, ys_n - k))

    first = (row * BAND).astype(F32)
    ypos = lax.broadcasted_iota(jnp.int32, (BAND, 128), 0).astype(F32) + first
    c1, s1 = fold_phase(ypos)
    yconst[0] = c1
    yconst[1] = s1
    yconst[2] = 2.0 * c1 * c1 - 1.0
    yconst[3] = 2.0 * s1 * c1

    ins[0].wait()
    ins[1].wait()
    sinfo[row, 8 * TAPS : 8 * TAPS + 4] = cell_ref[...].astype(F32)
    ins[7].wait()
    sinfo[row, 8 * TAPS + 4 : 8 * TAPS + 8] = dens_ref[...]

    pl.semaphore_wait(barrier, count)
    info = [None] + [
        remote(sinfo.at[row], sinfo.at[row], info_s.at[k], info_r.at[k], row_to=(row + k) % rows_n)
        for k in range(1, rows_n)
    ]

    def wide(tile):
        return jnp.concatenate([tile] * half, axis=1)

    def tables(k):
        band = (row + k) % rows_n
        cell = jnp.concatenate([sinfo[band, 8 * TAPS + b : 8 * TAPS + b + 1] for b in range(half)], axis=1)
        kxs = jnp.floor((cell + 0.5) * (1.0 / NXY))
        ky = cell - NXY * kxs
        k0, k1 = [
            [
                jnp.concatenate(
                    [sinfo[band, 8 * t + 2 * b + q : 8 * t + 2 * b + q + 1] for b in range(half)], axis=1
                )
                for t in range(TAPS)
            ]
            for q in range(2)
        ]
        cells = lax.broadcasted_iota(jnp.int32, (16, SAMP), 0).astype(F32)
        for g in range(8):
            if g < 7:
                offset = cells + (16.0 * g) - kxs
                weight = jnp.where(offset == 4.0, k1[4], 0.0)
                for t in range(3, -1, -1):
                    weight = jnp.where(offset == float(t), k1[t], weight)
                high, low = halves(weight)
            else:
                high = low = jnp.zeros((16, SAMP), BF16)
            cw[k, 16 * g : 16 * g + 16] = high
            cw[k, EXT + 16 * g : EXT + 16 * g + 16] = low
        low_pos = lax.broadcasted_iota(jnp.int32, (8, SAMP), 0).astype(F32)
        lo_c, lo_s = fold_phase(low_pos * ky)
        lo_c = lo_c * (1.0 / math.sqrt(NXY))
        lo_s = lo_s * (1.0 / math.sqrt(NXY))
        high_pos = lax.broadcasted_iota(jnp.int32, (16, SAMP), 0).astype(F32) * 8.0 + first
        hi_c, hi_s = fold_phase(high_pos * ky)
        even1, odd1 = k0[3] + k0[1], k0[3] - k0[1]
        even2, odd2 = k0[4] + k0[0], k0[4] - k0[0]
        for p in range(BAND // 8):
            r8 = slice(8 * p, 8 * p + 8)
            pr = k0[2] + even1 * wide(yconst[0, r8]) + even2 * wide(yconst[2, r8])
            pi = odd1 * wide(yconst[1, r8]) + odd2 * wide(yconst[3, r8])
            hc, hs = hi_c[p : p + 1], hi_s[p : p + 1]
            er = hc * lo_c - hs * lo_s
            es = hs * lo_c + hc * lo_s
            wr[k, 0, r8] = er * pr - es * pi
            wr[k, 1, r8] = er * pi + es * pr

    tables(0)

    ins[2].wait()
    ins[3].wait()
    for c in range(2):
        sr, si = sens_ref[0, c].astype(F32), sens_ref[1, c].astype(F32)
        dr, di = dir_ref[0], dir_ref[1]
        re_h, re_l = halves(sr * dr - si * di)
        im_h, im_l = halves(sr * di + si * dr)
        here = slice(c * BAND, (c + 1) * BAND)
        lhs_h[here, 0:NXY] = re_h
        lhs_h[here, NXY:] = im_h
        lhs_l[here, 0:NXY] = re_l
        lhs_l[here, NXY:] = im_l

    ins[4].wait()
    ins[5].wait()
    for copy in ins[9:]:
        copy.start()
    for band in range(rows_n):
        out = dot(lhs_h[...], fh_ref[band])
        out = out + dot(lhs_l[...], fh_ref[band])
        out = out + dot(lhs_h[...], fl_ref[band])
        high, low = halves(out)
        ke_h[band, 0:192] = high[:, :EXT]
        ke_h[band, 192:384] = high[:, EXT:]
        ke_l[band, 0:192] = low[:, :EXT]
        ke_l[band, 192:384] = low[:, EXT:]

    vals = {}
    for k in orders:
        band = (row + k) % rows_n
        if k:
            info[rows_n - k].wait_recv()
            tables(k)
        kh, kl = ke_h[band], ke_l[band]
        tbuf[...] = dot(jnp.concatenate([kh, kh], axis=1), cw[k]) + dot(kl, cw[k, 0:EXT])
        for c in range(2):
            vr = jnp.zeros((8, SAMP), F32)
            vi = jnp.zeros((8, SAMP), F32)
            for p in range(BAND // 8):
                tr = tbuf[c * BAND + 8 * p : c * BAND + 8 * p + 8]
                ti = tbuf[192 + c * BAND + 8 * p : 192 + c * BAND + 8 * p + 8]
                w_r, w_i = wr[k, 0, 8 * p : 8 * p + 8], wr[k, 1, 8 * p : 8 * p + 8]
                vr = vr + w_r * tr + w_i * ti
                vi = vi + w_r * ti - w_i * tr
            vr = jnp.sum(vr, axis=0, keepdims=True)
            vi = jnp.sum(vi, axis=0, keepdims=True)
            for b in range(half):
                vall[row, pair, band, c, b : b + 1] = vr[:, 128 * b : 128 * (b + 1)]
                vall[row, pair, band, c, half + b : half + b + 1] = vi[:, 128 * b : 128 * (b + 1)]
        for tk, e in eight:
            s, r = eight_to(tk, e)
            part = vall.at[row, pair, band]
            vals[k, tk, e] = remote(part, part, val_s.at[k, tk, e], val_r.at[k, tk, e], slab_to=s, row_to=r)

    def lanes(tile):
        folded = tile[:, 0:128] + tile[:, 128:256] + tile[:, 256:384]
        return jnp.sum(folded, axis=0, keepdims=True)

    ins[6].wait()
    dd = lanes(dir_ref[0] * dir_ref[0] + dir_ref[1] * dir_ref[1])
    rr = lanes(res_ref[0] * res_ref[0] + res_ref[1] * res_ref[1])
    scs[row, pair] = jnp.concatenate(
        [dd * (damping / coils), rr * (1.0 / coils), jnp.zeros((6, 128), F32)], axis=0
    )
    scc = []
    for k, e in eight:
        s, r = eight_to(k, e)
        scc.append(
            remote(scs.at[row, pair], scs.at[row, pair], sc_s.at[k, e], sc_r.at[k, e], slab_to=s, row_to=r)
        )

    power = jnp.zeros((8, 128), F32)
    for k in orders:
        band = (row + k) % rows_n
        for tk, e in eight:
            vals[(k + tk) % rows_n, tk, e].wait_recv()
        total = jnp.zeros((2, 8, 128), F32)
        for r in range(rows_n):
            for p in range(2):
                total = total + vall[r, p, band]
        value = 0.5 * total
        dens = sinfo[band, 8 * TAPS + 4 : 8 * TAPS + 8]
        weighted = value * jnp.concatenate([dens, dens], axis=0)[None]
        wall[band] = weighted
        power = power + weighted[0] * value[0] + weighted[1] * value[1]
        for c in range(2):
            w_re = jnp.concatenate([wall[band, c, b : b + 1] for b in range(half)], axis=1)
            w_im = jnp.concatenate([wall[band, c, half + b : half + b + 1] for b in range(half)], axis=1)
            for p in range(BAND // 16):
                m_r = wr[k, 0, 16 * p : 16 * p + 16]
                m_i = wr[k, 1, 16 * p : 16 * p + 16]
                re_h, re_l = halves(m_r * w_re - m_i * w_im)
                im_h, im_l = halves(m_r * w_im + m_i * w_re)
                here = slice(c * BAND + 16 * p, c * BAND + 16 * p + 16)
                there = slice(192 + c * BAND + 16 * p, 192 + c * BAND + 16 * p + 16)
                a_h[here] = re_h
                a_h[there] = im_h
                a_l[here] = re_l
                a_l[there] = im_l
        both = dot_nt(a_h[...], cw[k])
        out = both[:, :EXT] + both[:, EXT:] + dot_nt(a_l[...], cw[k, 0:EXT])
        high, low = halves(out)
        s_h[band, 0] = high[0:192]
        s_h[band, 1] = high[192:384]
        s_l[band, 0] = low[0:192]
        s_l[band, 1] = low[192:384]

    for copy in scc:
        copy.wait_recv()
    mine = jnp.zeros((8, 128), F32)
    for r in range(rows_n):
        for c in range(2):
            mine = mine + scs[r, c]
    curv = 2.0 * jnp.sum(power, axis=0, keepdims=True)
    mine = mine + jnp.concatenate([curv, jnp.zeros((7, 128), F32)], axis=0)

    def to_across(buf, send, recv):
        copies = []
        for k, e in across:
            s, c = across_to(k, e)
            copies.append(
                remote(buf.at[group, zl], buf.at[group, zl], send.at[k, e], recv.at[k, e], slab_to=s, coil_to=c)
            )
        return copies

    def total_of(buf, first, second):
        mine = jnp.zeros((8, 128), F32)
        for i in range(first):
            for j in range(second):
                mine = mine + buf[i, j]
        return mine

    g1[group, zl] = mine
    g1c = to_across(g1, g1_s, g1_r)

    left_h = jnp.concatenate([s_h[j, q] for j in range(rows_n) for q in range(2)], axis=1)
    left_l = jnp.concatenate([s_l[j, q] for j in range(rows_n) for q in range(2)], axis=1)
    other = (1 - zl) * ys_n + yy
    zrc = []
    ins[9].wait()
    ins[10].wait()
    for b in range(BLOCKS):
        out = dot(left_h, bh_ref[b]) + dot(left_l, bh_ref[b]) + dot(left_h, bl_ref[b])
        cols = slice(128 * b, 128 * (b + 1))
        term_r = dir_ref[0, :, cols] * (damping / coils)
        term_i = dir_ref[1, :, cols] * (damping / coils)
        for c in range(2):
            sr = sens_ref[0, c, :, cols].astype(F32)
            si = sens_ref[1, c, :, cols].astype(F32)
            br = out[c * BAND : (c + 1) * BAND, :128]
            bi = out[c * BAND : (c + 1) * BAND, 128:]
            term_r = term_r + sr * br + si * bi
            term_i = term_i + sr * bi - si * br
        for g in range(24):
            tz[b, 0, g] = term_r[4 * g : 4 * g + 4]
            tz[b, 1, g] = term_i[4 * g : 4 * g + 4]
        zrc.append(remote(tz.at[b, 1 - zl], zrecv.at[b], zr_s.at[b], zr_r.at[b], coil_to=other))
    for copy in g1c:
        copy.wait_recv()
    mine = total_of(g1, groups_n, 2)
    for i in range(ys_n):
        ysum[i, 36:40] = mine[0:4]
    for b in range(BLOCKS):
        zrc[b].wait_recv()
        for i in range(ys_n):
            for g in range(3):
                at = 12 * b + 4 * g
                ysum[i, at : at + 4] = tz[b, zl, 3 * i + g] + zrecv[b, 3 * i + g]
    yrc = []
    for k in reversed(near):
        to = (yy + k) % ys_n
        yrc.append(remote(ysum.at[to], yrecv.at[yy], yr_s.at[k], yr_r.at[k], coil_to=along_y(k)))
    yrecv[yy] = ysum[yy]
    drain()
    for copy in yrc:
        copy.wait_recv()
    piece = yrecv[0]
    for c in range(1, ys_n):
        piece = piece + yrecv[c]
    curvature = jnp.sum(piece[36:37], axis=1, keepdims=True)
    norm_now = jnp.sum(piece[37:38], axis=1, keepdims=True)
    step = norm_now / curvature

    left = jnp.zeros((12, 128), F32)
    for b in range(BLOCKS):
        rows = res_ref[zl, pl.ds(pl.multiple_of(8 * (12 * yy // 8), 8), 16), 128 * b : 128 * (b + 1)]
        own = jnp.where(yy % 2 == 1, rows[4:16], rows[0:12])
        gap = own - step * piece[12 * b : 12 * b + 12]
        left = left + gap * gap
    nb[coil, 0:36] = piece[0:36]
    nb[coil, 36:40] = jnp.zeros((4, 128), F32)
    e2[slab, row] = jnp.sum(left, axis=0, keepdims=True)
    e2c = [
        remote(e2.at[slab, row], e2.at[slab, row], e2_s.at[d, dr], e2_r.at[d, dr],
               slab_to=(slab + d) % slabs, row_to=(row + dr) % rows_n)
        for d, dr in wide_set
    ]
    yac = {
        k: remote(nb.at[coil], nb.at[coil], ya_s.at[k], ya_r.at[k], coil_to=along_y(k)) for k in near
    }

    def forward(k):
        part = nb.at[zl * ys_n + (yy - k + ys_n) % ys_n]
        return remote(part, part, za_s.at[k], za_r.at[k], coil_to=other)

    zac = [forward(0)]
    ins[8].wait()
    sol_buf[...] = sol_ref[...] + step * dir_ref[...]
    outs = [
        pltpu.make_async_copy(src, dst, out_sem.at[i])
        for i, (src, dst) in enumerate(((sol_buf, sol_out), (res_buf, res_out), (ratio_buf, ratio_out)))
    ]
    outs[0].start()
    for copy in e2c:
        copy.wait_recv()
    mine = jnp.zeros((1, 128), F32)
    for i in range(slabs):
        for r in range(rows_n):
            mine = mine + e2[i, r]
    c2[coil] = mine
    c2c = [
        remote(c2.at[coil], c2.at[coil], c2_s.at[k], c2_r.at[k], coil_to=(coil + k) % coils)
        for k in coil_set
    ]
    for k in near:
        yac[k].wait_recv()
        zac.append(forward(k))
    for copy in zac:
        copy.wait_recv()
    for b in range(BLOCKS):
        cols = slice(128 * b, 128 * (b + 1))
        for plane in range(2):
            for g in range(12):
                here = slice(8 * g, 8 * g + 8)
                parts = []
                for u in (2 * g, 2 * g + 1):
                    at = 12 * b + 4 * (u % 3)
                    parts.append(nb[plane * ys_n + u // 3, at : at + 4])
                normal = jnp.concatenate(parts, axis=0)
                res_buf[plane, here, cols] = res_ref[plane, here, cols] - step * normal
    outs[1].start()
    for copy in c2c:
        copy.wait_recv()
    folded = c2[0]
    for c in range(1, coils):
        folded = folded + c2[c]
    ratio = jnp.sum(folded, axis=1, keepdims=True) / norm_now
    ratio_buf[...] = jnp.broadcast_to(ratio, (8, 128))
    outs[2].start()
    drain()
    for copy in outs:
        copy.wait()


def put_kernel(
    sol_in, res_in, ratio_in, along_in, sol_out, res_out, dir_out,
    sol_buf, res_buf, ratio_buf, along_buf, dir_buf, load_sems, store_sems,
):
    loads = [
        pltpu.make_async_copy(src, dst, load_sems.at[i])
        for i, (src, dst) in enumerate((
            (res_in, res_buf), (ratio_in, ratio_buf), (along_in, along_buf), (sol_in, sol_buf),
        ))
    ]
    stores = [
        pltpu.make_async_copy(src, dst, store_sems.at[i])
        for i, (src, dst) in enumerate(((dir_buf, dir_out), (res_buf, res_out), (sol_buf, sol_out)))
    ]
    for copy in loads:
        copy.start()
    loads[0].wait()
    stores[1].start()
    loads[1].wait()
    loads[2].wait()
    dir_buf[...] = res_buf[...] + ratio_buf[0:1, 0:1] * along_buf[...]
    stores[0].start()
    loads[3].wait()
    stores[2].start()
    for copy in stores:
        copy.wait()


def on_device(tables, rows_n, groups_n, ys_n, solution, residual, direction, sens, sample_cell, kern, density):
    dma = pltpu.SemaphoreType.DMA
    vmem = pltpu.VMEM
    eight = (rows_n, 2)
    image = (2, BAND, NXY)
    scratch = [
        vmem(image, F32), vmem(image, F32), vmem(image, F32), vmem((2,) + image, BF16),
        vmem((4, 128), jnp.int32), vmem((4, 128), F32),
        vmem(tables[0].shape, BF16), vmem(tables[1].shape, BF16),
        vmem(tables[2].shape, BF16), vmem(tables[3].shape, BF16), dma((11,)),
        vmem(image, F32), vmem(image, F32), vmem((8, 128), F32), dma((3,)),
        vmem((192, 768), BF16), vmem((192, 768), BF16),
        vmem((rows_n, 384, EXT), BF16), vmem((rows_n, 384, EXT), BF16),
        vmem((rows_n, 48, 128), F32),
        vmem((rows_n, 2 * EXT, SAMP), BF16),
        vmem((rows_n, 2, BAND, SAMP), F32),
        vmem((384, SAMP), F32),
        vmem((4, BAND, 128), F32),
        vmem((384, SAMP), BF16), vmem((384, SAMP), BF16),
        vmem((rows_n, 2, 192, EXT), BF16), vmem((rows_n, 2, 192, EXT), BF16),
        vmem((rows_n, 2, rows_n, 2, 8, 128), F32), vmem((rows_n, 2, 8, 128), F32),
        vmem((rows_n, 2, 8, 128), F32),
        vmem((BLOCKS, 2, 24, 4, 128), F32), vmem((BLOCKS, 24, 4, 128), F32),
        vmem((ys_n, 40, 128), F32), vmem((ys_n, 40, 128), F32), vmem((2 * ys_n, 40, 128), F32),
        vmem((groups_n, 2, 8, 128), F32),
        vmem((2 * groups_n, rows_n, 1, 128), F32), vmem((2 * ys_n, 1, 128), F32),
    ]
    few, cross, ys, blocks = (rows_n,), (groups_n, 2), (ys_n,), (BLOCKS,)
    for shape in (few, (rows_n,) + eight, eight, cross, blocks, ys, (2 * groups_n, rows_n), ys, ys, (2 * ys_n,)):
        scratch.append(dma(shape))
        scratch.append(dma(shape))
    far = pl.BlockSpec(memory_space=pl.ANY)
    shapes = (jax.ShapeDtypeStruct(image, F32),) * 3
    taps = kern.reshape(2, TAPS, 4, 128).transpose(1, 2, 0, 3).reshape(8 * TAPS, 128)
    outs = pl.pallas_call(
        functools.partial(kernel, rows_n, groups_n, ys_n),
        out_shape=shapes[:2] + (jax.ShapeDtypeStruct((8, 128), F32),),
        in_specs=[far] * 11,
        out_specs=(far,) * 3,
        scratch_shapes=scratch,
        compiler_params=pltpu.CompilerParams(
            collective_id=0, has_side_effects=True, vmem_limit_bytes=56000 * 1024
        ),
    )(
        direction[:, 0], residual[:, 0], solution[:, 0], sens[:, :, 0],
        sample_cell.reshape(4, 128), taps, density.reshape(4, 128), *tables,
    )
    outs = pl.pallas_call(
        put_kernel,
        out_shape=shapes,
        in_specs=[far] * 4,
        out_specs=(far,) * 3,
        scratch_shapes=[vmem(image, F32)] * 2 + [vmem((8, 128), F32)] + [vmem(image, F32)] * 2 + [dma((4,)), dma((3,))], compiler_params=pltpu.CompilerParams(vmem_limit_bytes=56000 * 1024),
    )(*outs, direction[:, 0])
    return tuple(out[:, None] for out in outs)


def solution(mesh):
    rows_n = mesh.shape["row"]
    groups_n = mesh.shape["slab"] // 2
    ys_n = mesh.shape["coil"] // 2
    tables = transform_tables(rows_n)

    def whole(*args):
        return on_device([jnp.asarray(t) for t in tables], rows_n, groups_n, ys_n, *args)

    image = P(None, "slab", "row", None)
    return jax.shard_map(
        whole,
        mesh=mesh,
        in_specs=(
            image, image, image, P(None, "coil", "slab", "row", None),
            P("row"), P(None, None, "row"), P("row"),
        ),
        out_specs=(image, image, image),
        check_vma=False,
    )
```
